256 devices in a mesh: grp: 2 (over z_hi), fsdp: 128 (over z_lo, y, x, core).
Axes of the slice: x: 4, y: 4, z: 8 (z_hi: 2, z_lo: 4; z = z_hi * 4 + z_lo), core: 2. Of those that a mesh axis runs over, the one named last changes fastest.
Arguments:
- hidden_act: bfloat16 [131072, 1024], P(('grp', 'fsdp')), may hold values from -24 to 24
- out_grad: bfloat16 [131072, 1024], P(('grp', 'fsdp')), may hold values from -0.015625 to 0.015625
- layer_stats: float32 [4096, 512], P(('grp', 'fsdp')), may hold values from -4 to 4
- resident_stats: float32 [1024, 512, 512], P(('grp', 'fsdp')), as said below
- slot_block: int32 [1024], replicated, may hold values from 0 to 1023, as said below
- layer_refresh: int32 [64], replicated, may hold values from 0 to 1, as said below
Outputs:
- grad_shard: float32 [1024, 1024], P(('grp', 'fsdp'))
- stats_new: float32 [4096, 512], P(('grp', 'fsdp'))
- pair_roots: float32 [256, 512, 512], P(('grp', 'fsdp'))
The draws below stay inside these ranges and needn't reach their ends.
Inputs may be any that keep to these rules, and one draw needn't show every extreme that they name: slot_block is a permutation of the 1024 block numbers; block b belongs to layer b // 16; for every fsdp index the 8 slots of its two devices (one of each group) hold exactly two blocks whose layer is refreshed; at some fsdp index both lie on the device of group 0, at some other both on the device of group 1. `layer_refresh`: a quarter of the 64 layers are 1. `resident_stats`: every block is symmetric positive definite.
All inputs are finite; a program needn't handle non-finite values.
Results may differ from the reference program's by a relative error of at most 0.0003.
Values sent between devices are 32-bit elements; how exact they have to be, the bound alone decides.
A program may use at most 64 MiB of HBM per device.

```python
import jax
import jax.numpy as jnp
from jax import lax

BLK = 512
TR = 2
TC = 2
SLOTS_PER_DEVICE = 4
BPL = 16
ITERS = 3
KW = 1024
DW = 1024
TOKENS = 131072
TOTAL_STAT_SLOTS = 1024
LAYERS = 64
N_GRP = 2
N_FSDP = 128


def stagger_plan(key):
    block_pairs = TOTAL_STAT_SLOTS // 8
    layer_key, fresh_random_key, stale_random_key, place_key, pick_key = jax.random.split(key, 5)
    layer_order = jax.random.permutation(layer_key, LAYERS)
    refresh = jnp.zeros((LAYERS,), jnp.int32).at[layer_order[:LAYERS // 4]].set(1)
    statistic_blocks = jnp.arange(TOTAL_STAT_SLOTS, dtype=jnp.int32)
    marked = refresh[statistic_blocks // BPL]
    ranked_blocks = jnp.argsort(1 - marked, stable=True).astype(jnp.int32)
    fresh_roots = jax.random.permutation(fresh_random_key, ranked_blocks[:TOTAL_STAT_SLOTS // 4]).reshape(block_pairs, 2)
    stale_roots = jax.random.permutation(stale_random_key, ranked_blocks[TOTAL_STAT_SLOTS // 4:]).reshape(block_pairs, 6)
    combined = jnp.concatenate([fresh_roots, stale_roots], axis=1)
    place_keys = jax.random.split(place_key, block_pairs)
    spots = jax.vmap(lambda single_block: jax.random.permutation(single_block, 8))(place_keys)
    picked_pairs = jax.random.permutation(pick_key, block_pairs)[:2]
    pair_numbers = jnp.arange(block_pairs, dtype=jnp.int32)
    lower_spots = jnp.array([0, 1, 2, 3, 4, 5, 6, 7], jnp.int32)
    upper_spots = jnp.array([2, 3, 4, 5, 0, 1, 6, 7], jnp.int32)
    spots = jnp.where((pair_numbers == picked_pairs[0])[:, None], lower_spots[None, :], spots)
    spots = jnp.where((pair_numbers == picked_pairs[1])[:, None], upper_spots[None, :], spots)
    placed_blocks = jnp.take_along_axis(combined, spots, axis=1)
    resident_slots = placed_blocks.reshape(block_pairs, 2, 4).transpose(1, 0, 2).reshape(TOTAL_STAT_SLOTS)
    return (resident_slots.astype(jnp.int32), refresh)


def draw_slot_block(key, part):
    resident_slots, refresh = stagger_plan(key)
    return resident_slots


def draw_layer_refresh(key, part):
    resident_slots, refresh = stagger_plan(key)
    return refresh


def draw_resident_stats(key, part):
    key = jax.random.fold_in(key, 7)
    spread = jnp.log(10.0)
    identity = jnp.eye(BLK, dtype=jnp.float32)
    reach = jnp.sqrt(3.0)

    def single_block(block_key):
        raw_key, scale_key = jax.random.split(block_key)
        factor = jax.random.uniform(raw_key, (BLK, BLK), jnp.float32, -reach, reach)
        gram = jnp.matmul(factor, factor.T, precision=lax.Precision.HIGHEST) / BLK
        gram = 0.5 * (gram + gram.T)
        scales = jnp.exp(0.5 * spread * jax.random.uniform(scale_key, (BLK,), jnp.float32))
        core = gram + 0.3 * identity
        return core * scales[:, None] * scales[None, :]
    return lax.map(single_block, jax.random.split(key, TOTAL_STAT_SLOTS))


def raised(result, stream_key, source, target, blocks, factor):
    owner, partner = [(jnp.arange(result.shape[dim]) // (result.shape[dim] // blocks)).reshape([-1 if axis == dim else 1 for axis in range(result.ndim)]) for dim in (source, target)]
    chosen = jax.random.permutation(stream_key, blocks)[partner]
    strong = (owner == chosen) | (owner == (partner + blocks // 2) % blocks)
    return jnp.where(strong, factor * result, result)


def steps_of(key, shape, cuts, smallest, largest):
    def one(position, blocks):
        steps = jax.random.uniform(jax.random.fold_in(jax.random.fold_in(key, 6), position), (blocks,), jnp.float32, smallest / len(cuts), largest / len(cuts))
        return jnp.repeat(jnp.exp(steps), shape[position] // blocks).reshape((-1,) + (1,) * (len(shape) - position - 1))

    factor_of = one(*cuts[0])
    for cut in cuts[1:]:
        factor_of = factor_of * one(*cut)
    return factor_of


def gaussian(rng, extent, scale, bound, cuts=(), kind=jnp.bfloat16):
    entries = scale * jax.random.normal(rng, extent, jnp.float32)
    if cuts:
        entries = entries * steps_of(rng, extent, cuts, -0.22, 0.18)
    return jnp.clip(entries, -bound, bound).astype(kind)


def bell_draw_with(rng, shape, deviation, limit, shards, heavy, held_as=jnp.bfloat16):
    values = deviation * jax.random.normal(rng, shape, jnp.float32)
    if shards:
        values = values * steps_of(rng, shape, shards, -0.22, 0.18)
    return jnp.clip(raised(values, jax.random.fold_in(rng, 3), *heavy), -limit, limit).astype(held_as)


def setup_inputs(seed: int = 0) -> dict:
    splits = jax.random.split(jax.random.key(seed), 7)
    return {
        "hidden_act": bell_draw_with(splits[0], (TOKENS, KW), 1.0, 24.0, ((0, 256),), (0, 1, 256, 6.0)),
        "out_grad": gaussian(splits[1], (TOKENS, DW), TOKENS ** -0.5, 0.015625, ((0, 256),)),
        "layer_stats": gaussian(splits[2], (2 * TR * TC * BLK, BLK), 0.5, 4.0, ((0, 256),), jnp.float32),
        "resident_stats": draw_resident_stats(jax.random.fold_in(splits[6], 71), 0),
        "slot_block": draw_slot_block(jax.random.fold_in(splits[6], 71), 0),
        "layer_refresh": draw_layer_refresh(jax.random.fold_in(splits[6], 71), 0),
    }


EPSILON = 0.0001
HIGHEST = lax.Precision.HIGHEST

def fourth_root(stat):
    identity = jnp.eye(stat.shape[-1], dtype=stat.dtype)
    matrix = stat + EPSILON * identity
    magnitude = jnp.sqrt(lax.optimization_barrier(jnp.sum(matrix * matrix, axis=(-2, -1), keepdims=True)) + 1e-06)
    scaling = 2.5 / magnitude
    moving = scaling * matrix
    iterate = jnp.sqrt(jnp.sqrt(scaling)) * identity
    for number in range(ITERS):
        factor = (5.0 * identity - moving) * 0.25
        iterate = jnp.matmul(iterate, factor, precision=HIGHEST)
        square = jnp.matmul(factor, factor, precision=HIGHEST)
        fourth = jnp.matmul(square, square, precision=HIGHEST)
        moving = jnp.matmul(fourth, moving, precision=HIGHEST)
    return iterate

def reference(hidden_act, out_grad, layer_stats, resident_stats, slot_block, layer_refresh):
    grad_shard = jnp.dot(hidden_act.T, out_grad, preferred_element_type=jnp.float32)
    pieces = []
    for row_tile in range(TR):
        for col_tile in range(TC):
            block = grad_shard[row_tile * BLK:(row_tile + 1) * BLK, col_tile * BLK:(col_tile + 1) * BLK]
            pieces.append(jnp.dot(block, block.T, precision=HIGHEST) / BLK)
            pieces.append(jnp.dot(block.T, block, precision=HIGHEST) / BLK)
    stats_new = layer_stats + jnp.concatenate(pieces, axis=0)
    flags = layer_refresh[slot_block // BPL]
    slot_ordering = jnp.arange(TOTAL_STAT_SLOTS, dtype=jnp.int32).reshape(N_GRP, N_FSDP, SLOTS_PER_DEVICE)
    slot_ordering = slot_ordering.transpose(1, 0, 2).reshape(N_FSDP, N_GRP * SLOTS_PER_DEVICE)
    marks = flags[slot_ordering]
    ranks = jnp.cumsum(marks, axis=1, dtype=jnp.int32) - 1
    first_pick = lax.optimization_barrier(jnp.sum(slot_ordering * marks * (ranks == 0).astype(jnp.int32), axis=1, dtype=jnp.int32))
    second_pick = lax.optimization_barrier(jnp.sum(slot_ordering * marks * (ranks == 1).astype(jnp.int32), axis=1, dtype=jnp.int32))
    chosen = jnp.stack([first_pick, second_pick], axis=0).reshape(2 * N_FSDP)
    pair_roots = lax.map(lambda slot: fourth_root(resident_stats[slot]), chosen)
    return (grad_shard, stats_new, pair_roots)
```

```python
import jax
import jax.numpy as jnp
from jax import lax
from jax.experimental import pallas as pl
from jax.experimental.pallas import tpu as pltpu
from jax.sharding import PartitionSpec as P

BPL = 16
EPSILON = 0.0001
MESH = pl.DeviceIdType.MESH
F32 = jnp.float32
BF16 = jnp.bfloat16
ZL, NY, NX, NZ = 4, 4, 4, 8
BLK = 512
HALF = 256
ROWS = 256


def split(value):
    high = value.astype(BF16)
    return high, (value - high.astype(F32)).astype(BF16)


def dot(a, b, dims=(((1,), (0,)), ((), ()))):
    return lax.dot_general(a, b, dims, preferred_element_type=F32)


def kernel(
    hid_any, og_any, stats_in, res_any, slot_block, refresh,
    grad_out, stats_out, root_out,
    hid, og, res, g_send, g_own, core_recv, p1a, p1b, a1, b1, p2a, p2b, r, p3, fin, fin_other,
    tile, t_high, t_low, wide, pack, pack_recv,
    m0, m0_h, m0_l, q_h, q_l, r_h, r_l, w_h, w_l, p_f, p_h, p_l,
    in_sem, send_sem, recv_sem,
):
    grp = lax.axis_index("grp")
    f = lax.axis_index("fsdp")
    zl = f // 32
    y = (f // 8) % NY
    x = (f // 2) % NX
    c = f % 2
    z = grp * ZL + zl
    active = c == zl // 2

    def dev(z_, y_, x_, c_):
        return (z_ // ZL, (z_ % ZL) * 32 + y_ * 8 + x_ * 2 + c_)

    partner = dev(z, y, x, 1 - c)
    xs = [dev(z, y, (x + k) % NX, c) for k in range(1, NX)]
    ys = [dev(z, (y + k) % NY, x, c) for k in range(1, NY)]
    zs = [dev((z + k) % NZ, y, x, c) for k in range(1, NZ)]

    sends = iter(range(100))
    recvs = iter(range(100))

    def copy(src, dst, to, recv=None):
        s = send_sem.at[next(sends)]
        return pltpu.make_async_remote_copy(
            src_ref=src, dst_ref=dst, send_sem=s,
            recv_sem=recv_sem.at[next(recvs)] if recv is None else recv,
            device_id=to, device_id_type=MESH,
        )

    loads = [
        pltpu.make_async_copy(src, dst, in_sem.at[i])
        for i, (src, dst) in enumerate([(og_any, og), (hid_any, hid), (res_any, res)])
    ]
    for load in loads:
        load.start()
    barrier = pltpu.get_barrier_semaphore()
    peers = [partner] + xs + ys + zs
    for peer in peers:
        pl.semaphore_signal(barrier, inc=1, device_id=peer, device_id_type=MESH)

    own = (grp * 128 + f) * 4
    flags = [refresh[slot_block[own + l] // BPL] for l in range(4)]
    count = flags[0] + flags[1] + flags[2] + flags[3]
    pick0 = jnp.int32(0)
    pick1 = jnp.int32(0)
    before = jnp.int32(0)
    for l in range(4):
        pick0 = pick0 + jnp.where(before == 0, flags[l], 0) * l
        pick1 = pick1 + jnp.where(before == 1, flags[l], 0) * l
        before = before + flags[l]
    send_pick = jnp.where(grp == 0, pick1, pick0)
    own_pick = jnp.where(jnp.logical_and(grp == 1, count == 2), pick1, pick0)
    use_recv = count == 0

    def grad_part(dst, half):
        columns = pl.ds(pl.multiple_of(half * BLK, BLK), BLK)

        def step(i, carry):
            rows = pl.ds(pl.multiple_of(i * ROWS, ROWS), ROWS)
            part = dot(hid[:, rows], og[:, columns], (((0,), (0,)), ((), ())))
            dst[pl.ds(i * 2, 2)] = part.reshape(2, NY, NX, 8, BLK)
            return carry

        lax.fori_loop(0, 1024 // ROWS, step, 0)

    loads[0].wait()
    loads[1].wait()
    grad_part(g_send, 1 - c)

    loads[2].wait()
    row = lax.broadcasted_iota(jnp.int32, (HALF, HALF), 0)
    col = lax.broadcasted_iota(jnp.int32, (HALF, HALF), 1)
    lower_block = res[send_pick, HALF:, HALF:]
    pack[0:HALF] = res[send_pick, :HALF, HALF:]
    pack[HALF:2 * HALF] = jnp.where(row <= col, res[send_pick, :HALF, :HALF], lower_block)
    diagonal = jnp.sum(jnp.where(row == col, lower_block, 0.0), axis=0, keepdims=True)
    pack[2 * HALF:2 * HALF + 8] = jnp.broadcast_to(diagonal, (8, HALF))

    pl.semaphore_wait(barrier, len(peers))

    core = [copy(g_send.at[pl.ds(4 * i, 4)], core_recv.at[pl.ds(4 * i, 4)], partner) for i in range(2)]
    for item in core:
        item.start()
    exchange = copy(pack, pack_recv, zs[3])
    exchange.start()
    grad_part(g_own, c)

    phase1 = []
    for i, (axis_peers, buf) in enumerate(((xs, p1a), (ys, p1b))):
        core[i].wait_recv()

        def add(j, carry, i=i):
            g_own[4 * i + j] += core_recv[4 * i + j]
            return carry

        lax.fori_loop(0, 4, add, 0)
        group = []
        for k in range(1, 4):
            src = g_own.at[pl.ds(0, 4), :, (x + k) % NX] if i == 0 else g_own.at[pl.ds(4, 4), (y + k) % NY]
            group.append(copy(src, buf.at[k - 1], axis_peers[k - 1]))
            group[-1].start()
        phase1.append(group)
    phase2 = []
    for i, (axis_peers, buf, got, total) in enumerate(((ys, p2a, p1a, a1), (xs, p2b, p1b, b1))):
        for item in phase1[i]:
            item.wait_recv()

        def add(j, carry, i=i, got=got, total=total):
            mine = g_own[j, :, x] if i == 0 else g_own[4 + j, y]
            total[j] = mine + got[0, j] + got[1, j] + got[2, j]
            return carry

        lax.fori_loop(0, 4, add, 0)
        group = []
        for k in range(1, 4):
            at = (y + k) % NY if i == 0 else (x + k) % NX
            group.append(copy(total.at[:, at], buf.at[k - 1], axis_peers[k - 1]))
            group[-1].start()
        phase2.append(group)
    for i, (got, total, at) in enumerate(((p2a, a1, y), (p2b, b1, x))):
        for item in phase2[i]:
            item.wait_recv()
        r[4 * i:4 * i + 4] = total[:, at] + got[0] + got[1] + got[2]
    phase3 = []
    for k in range(1, NZ):
        phase3.append(copy(r.at[(z + k) % NZ], p3.at[k - 1], zs[k - 1]))
        phase3[-1].start()
    for item in phase3:
        item.wait_recv()
    mine = r[z]
    for k in range(7):
        mine = mine + p3[k]
    fin[...] = mine

    swap = copy(fin, fin_other, partner)
    swap.start()

    gz_base = [next(recvs) for _ in range(4)][0]
    gz = []
    for t in range(2):
        to = 2 * c + t
        item = copy(
            fin, tile.at[zl, y, x], dev(grp * ZL + to, y, x, c), recv_sem.at[gz_base + zl]
        )
        pl.when(to != zl)(item.start)
        gz.append((to != zl, item))

    def gather_z():
        tile[zl, y, x] = mine
        for k in range(1, 4):
            source = (zl + k) % ZL
            pltpu.make_async_remote_copy(
                src_ref=fin, dst_ref=tile.at[source, y, x], send_sem=send_sem.at[0],
                recv_sem=recv_sem.at[gz_base + source], device_id=partner, device_id_type=MESH,
            ).wait_recv()

    pl.when(active)(gather_z)

    def pair(k, i, stage):
        if stage == 1:
            return (tile.at[pl.ds(0, 2), y, x], ys[k - 1]) if i == 0 else (tile.at[pl.ds(2, 2), y, x], xs[k - 1])
        return (tile.at[pl.ds(0, 2), :, x], xs[k - 1]) if i == 0 else (tile.at[pl.ds(2, 2), y], ys[k - 1])

    stages = []
    for stage in (1, 2):
        stages.append([[copy(*(lambda s, d: (s, s, d))(*pair(k, i, stage))) for k in range(1, 4)] for i in range(2)])
    slabs = [
        [tile.at[pl.ds(0, 2), :, (x + 4 - k) % NX] for k in range(4)],
        [tile.at[pl.ds(2, 2), (y + 4 - k) % NY] for k in range(4)],
    ]
    forward = [[copy(slabs[i][k], slabs[i][k], partner) for k in range(4)] for i in range(2)]

    def gather_plane():
        for group in stages[0]:
            for item in group:
                item.start()
        for i in range(2):
            for k, item in enumerate(stages[0][i]):
                item.wait_recv()
            for item in stages[1][i]:
                item.start()
            forward[i][0].start()
        for k in range(1, 4):
            for i in range(2):
                stages[1][i][k - 1].wait_recv()
                forward[i][k].start()
        for stage in stages:
            for group in stage:
                for item in group:
                    item.wait_send()
        for group in forward:
            for item in group:
                item.wait_send()

    pl.when(active)(gather_plane)

    def take_forward():
        for i in range(2):
            for k in range(4):
                forward[i][k].wait_recv()

    pl.when(jnp.logical_not(active))(take_forward)

    swap.wait_recv()
    low = jnp.where(c == 0, fin[...], fin_other[...])
    high = jnp.where(c == 0, fin_other[...], fin[...])
    grad_out[:, :BLK] = jnp.where(c == 0, low[:4], low[4:])
    grad_out[:, BLK:] = jnp.where(c == 0, high[:4], high[4:])

    t_value = tile[...].reshape(BLK, BLK)
    t_h, t_l = split(t_value)
    t_high[...] = t_h
    t_low[...] = t_l
    at = (f % 32) * 16

    def left():
        dims = (((1,), (1,)), ((), ()))
        rows = pl.ds(pl.multiple_of(at, 16), 16)
        lead_h, lead_l = t_high[rows, :], t_low[rows, :]
        part = dot(lead_h, t_high[...], dims) + dot(lead_h, t_low[...], dims) + dot(lead_l, t_high[...], dims)
        stats_out[...] = stats_in[...] + part * (1.0 / BLK)

    def right():
        dims = (((0,), (0,)), ((), ()))
        columns = pl.ds(pl.multiple_of(at // 128 * 128, 128), 128)
        lead_h, lead_l = t_high[:, columns], t_low[:, columns]
        wide[...] = dot(lead_h, t_high[...], dims) + dot(lead_h, t_low[...], dims) + dot(lead_l, t_high[...], dims)
        part = wide[pl.ds(pl.multiple_of(at % 128, 16), 16), :]
        stats_out[...] = stats_in[...] + part * (1.0 / BLK)

    pl.when(zl % 2 == 0)(left)
    pl.when(zl % 2 == 1)(right)

    exchange.wait_recv()
    eye = (row == col).astype(F32)
    upper = pack_recv[HALF:2 * HALF]
    flipped = upper.T
    off = pack_recv[0:HALF]
    block_a = jnp.where(row <= col, upper, flipped)
    block_d = jnp.where(row > col, upper, flipped)
    block_d = jnp.where(row == col, jnp.broadcast_to(pack_recv[2 * HALF:2 * HALF + 1], (HALF, HALF)), block_d)
    total = jnp.zeros((1, 1), F32)
    for i, j, got in ((0, 0, block_a), (0, 1, off), (1, 0, off.T), (1, 1, block_d)):
        rows, cols = pl.ds(i * HALF, HALF), pl.ds(j * HALF, HALF)
        value = jnp.where(use_recv, got, res[own_pick, rows, cols])
        if i == j:
            value = value + EPSILON * eye
        m0[rows, cols] = value
        total = total + jnp.sum(value * value, axis=(0, 1), keepdims=True)
    zeta = 2.5 / jnp.sqrt(total + 1e-06)
    scale = jnp.sqrt(jnp.sqrt(zeta))

    def blocks(body):
        def step(i, carry):
            body(i, pl.ds(pl.multiple_of(i * ROWS, ROWS), ROWS))
            return carry
        lax.fori_loop(0, BLK // ROWS, step, 0)

    def put(high, low, rows, value):
        value_h, value_l = split(value)
        high[rows, :] = value_h
        low[rows, :] = value_l

    def product(ah, al, bh, bl, rows):
        lead = ah[rows, :]
        return dot(lead, bh[...]) + dot(lead, bl[...]) + dot(al[rows, :], bh[...])

    def ident(i):
        r_ = lax.broadcasted_iota(jnp.int32, (ROWS, BLK), 0) + i * ROWS
        c_ = lax.broadcasted_iota(jnp.int32, (ROWS, BLK), 1)
        return (r_ == c_).astype(F32)

    def step0(i, rows):
        value = m0[rows, :] * zeta
        m0[rows, :] = value
        put(m0_h, m0_l, rows, value)

    def step1(i, rows):
        square = product(m0_h, m0_l, m0_h, m0_l, rows)
        m = m0[rows, :]
        put(w_h, w_l, rows, (5.0 * m - square) * 0.25)
        put(q_h, q_l, rows, (25.0 * ident(i) - 10.0 * m + square) * 0.0625)

    def step2(i, rows):
        put(r_h, r_l, rows, product(q_h, q_l, q_h, q_l, rows))

    def step3(i, rows):
        fifth = product(r_h, r_l, w_h, w_l, rows)
        factor = (5.0 * ident(i) - m0[rows, :]) * 0.25
        value = (5.0 * factor - fifth) * 0.25
        p_f[rows, :] = value
        put(p_h, p_l, rows, value)

    def step4(i, rows):
        put(q_h, q_l, rows, product(p_h, p_l, p_h, p_l, rows))

    def step5(i, rows):
        put(w_h, w_l, rows, product(p_h, p_l, m0_h, m0_l, rows))

    def step6(i, rows):
        fifth = product(r_h, r_l, w_h, w_l, rows)
        root_out[0, rows, :] = (5.0 * p_f[rows, :] - fifth) * (0.25 * scale)

    for body in (step0, step1, step2, step3, step4, step5, step2, step6):
        blocks(body)

    for item in core + [exchange, swap] + phase1[0] + phase1[1] + phase2[0] + phase2[1] + phase3:
        item.wait_send()
    for sent, item in gz:
        pl.when(sent)(item.wait_send)


def on_device(hidden_act, out_grad, layer_stats, resident_stats, slot_block, layer_refresh):
    vmem = pl.BlockSpec(memory_space=pltpu.VMEM)
    anywhere = pl.BlockSpec(memory_space=pl.ANY)
    smem = pl.BlockSpec(memory_space=pltpu.SMEM)
    square = (BLK, BLK)
    piece = (8, BLK)
    scratch = [
        pltpu.VMEM(hidden_act.shape, BF16),
        pltpu.VMEM(out_grad.shape, BF16),
        pltpu.VMEM(resident_stats.shape, F32),
        pltpu.VMEM((NZ, NY, NX) + piece, F32),
        pltpu.VMEM((NZ, NY, NX) + piece, F32),
        pltpu.VMEM((NZ, NY, NX) + piece, F32),
        pltpu.VMEM((3, 4, NY) + piece, F32),
        pltpu.VMEM((3, 4, NX) + piece, F32),
        pltpu.VMEM((4, NY) + piece, F32),
        pltpu.VMEM((4, NX) + piece, F32),
        pltpu.VMEM((3, 4) + piece, F32),
        pltpu.VMEM((3, 4) + piece, F32),
        pltpu.VMEM((NZ,) + piece, F32),
        pltpu.VMEM((7,) + piece, F32),
        pltpu.VMEM(piece, F32),
        pltpu.VMEM(piece, F32),
        pltpu.VMEM((ZL, NY, NX) + piece, F32),
        pltpu.VMEM(square, BF16),
        pltpu.VMEM(square, BF16),
        pltpu.VMEM((128, BLK), F32),
        pltpu.VMEM((2 * HALF + 8, HALF), F32),
        pltpu.VMEM((2 * HALF + 8, HALF), F32),
        pltpu.VMEM(square, F32),
        pltpu.VMEM(square, BF16),
        pltpu.VMEM(square, BF16),
        pltpu.VMEM(square, BF16),
        pltpu.VMEM(square, BF16),
        pltpu.VMEM(square, BF16),
        pltpu.VMEM(square, BF16),
        pltpu.VMEM(square, BF16),
        pltpu.VMEM(square, BF16),
        pltpu.VMEM(square, F32),
        pltpu.VMEM(square, BF16),
        pltpu.VMEM(square, BF16),
        pltpu.SemaphoreType.DMA((3,)),
        pltpu.SemaphoreType.DMA((64,)),
        pltpu.SemaphoreType.DMA((64,)),
    ]
    return pl.pallas_call(
        kernel,
        out_shape=(
            jax.ShapeDtypeStruct((4, 1024), F32),
            jax.ShapeDtypeStruct(layer_stats.shape, F32),
            jax.ShapeDtypeStruct((1, BLK, BLK), F32),
        ),
        in_specs=[anywhere, anywhere, vmem, anywhere, smem, smem],
        out_specs=(vmem, vmem, vmem),
        scratch_shapes=scratch,
        compiler_params=pltpu.CompilerParams(
            collective_id=0, has_side_effects=True, vmem_limit_bytes=48 * 1024 * 1024
        ),
        cost_estimate=pl.CostEstimate(flops=10**10, bytes_accessed=10**7, transcendentals=0),
    )(hidden_act, out_grad, layer_stats, resident_stats, slot_block, layer_refresh)


def solution(mesh):
    in_specs = (
        P(("grp", "fsdp"), None),
        P(("grp", "fsdp"), None),
        P(("grp", "fsdp"), None),
        P(("grp", "fsdp"), None, None),
        P(),
        P(),
    )
    out_specs = (P(("grp", "fsdp"), None), P(("grp", "fsdp"), None), P(("grp", "fsdp"), None, None))
    return jax.shard_map(
        on_device, mesh=mesh, in_specs=in_specs, out_specs=out_specs, check_vma=False
    )
```

```python
import jax
import jax.numpy as jnp
from jax import lax
from jax.experimental import pallas as pl
from jax.experimental.pallas import tpu as pltpu
from jax.sharding import PartitionSpec as P

BPL = 16
EPSILON = 0.0001
MESH = pl.DeviceIdType.MESH
F32 = jnp.float32
BF16 = jnp.bfloat16
ZL, NY, NX, NZ = 4, 4, 4, 8
BLK = 512
HALF = 256
ROWS = 256
NCH = 2
PC = 4 // NCH
LAG = 2
HOOKS = (3, 3, 3, 3, 3)
SEMS = 100


def split(value):
    high = value.astype(BF16)
    return high, (value - high.astype(F32)).astype(BF16)


def dot(a, b, dims=(((1,), (0,)), ((), ()))):
    return lax.dot_general(a, b, dims, preferred_element_type=F32)


def kernel(
    hid_any, og_any, stats_any, res_any, slots_any, refresh_any,
    grad_out, stats_out, root_out,
    hid, og, stats_in, res, slot_block, refresh,
    g_send, g_own, core_recv, p1a, p1b, a1, b1, p2a, p2b, r, p3, fin, fin_other,
    tile, t_high, t_low, wide, pack, pack_recv,
    m0, m0_h, m0_l, q_h, q_l, r_h, r_l, w_h, w_l, p_f, p_h, p_l,
    in_sem, send_sem, recv_sem,
):
    grp = lax.axis_index("grp")
    f = lax.axis_index("fsdp")
    zl = f // 32
    y = (f // 8) % NY
    x = (f // 2) % NX
    c = f % 2
    z = grp * ZL + zl

    def dev(z_, y_, x_, c_):
        return (z_ // ZL, (z_ % ZL) * 32 + y_ * 8 + x_ * 2 + c_)

    partner = dev(z, y, x, 1 - c)
    xs = [dev(z, y, (x + k) % NX, c) for k in range(1, NX)]
    ys = [dev(z, (y + k) % NY, x, c) for k in range(1, NY)]
    zs = [dev((z + k) % NZ, y, x, c) for k in range(1, NZ)]

    sends = iter(range(SEMS))
    recvs = iter(range(SEMS))

    def copy(src, dst, to, recv=None):
        return pltpu.make_async_remote_copy(
            src_ref=src, dst_ref=dst, send_sem=send_sem.at[next(sends)],
            recv_sem=recv_sem.at[next(recvs)] if recv is None else recv,
            device_id=to, device_id_type=MESH,
        )

    barrier = pltpu.get_barrier_semaphore()
    peers = [partner] + xs + ys + zs
    cross = [dev(grp * ZL + (zl + k) % ZL, y, x, 1 - c) for k in range(1, ZL)]
    peers = peers + cross
    for peer in peers:
        pl.semaphore_signal(barrier, inc=1, device_id=peer, device_id_type=MESH)
    loads = [
        pltpu.make_async_copy(src, dst, in_sem.at[i])
        for i, (src, dst) in enumerate([
            (og_any, og), (hid_any, hid), (slots_any, slot_block), (refresh_any, refresh),
            (res_any, res), (stats_any, stats_in),
        ])
    ]
    for load in loads:
        load.start()

    def planes(i, j):
        return 4 * i + j * PC

    def grad_part(i, j, half):
        rows = pl.ds(planes(i, j) * 128, PC * 128)
        columns = pl.ds(pl.multiple_of(half * BLK, BLK), BLK)
        part = dot(hid[:, rows], og[:, columns], (((0,), (0,)), ((), ())))
        return part.reshape(PC, NY, NX, 8, BLK)

    chunks = [(i, j) for j in range(NCH) for i in range(2)]

    loads[0].wait()
    loads[1].wait()
    core = {}
    for n, (i, j) in enumerate(chunks):
        at = pl.ds(planes(i, j), PC)
        g_send[at] = grad_part(i, j, 1 - c)
        if n == 0:
            pl.semaphore_wait(barrier, len(peers))
        core[i, j] = copy(g_send.at[at], core_recv.at[at], partner)
        core[i, j].start()

    for load in loads[2:]:
        load.wait()
    own = (grp * 128 + f) * 4
    flags = [refresh[slot_block[own + l] // BPL] for l in range(4)]
    count = flags[0] + flags[1] + flags[2] + flags[3]
    pick0 = jnp.int32(0)
    pick1 = jnp.int32(0)
    before = jnp.int32(0)
    for l in range(4):
        pick0 = pick0 + jnp.where(before == 0, flags[l], 0) * l
        pick1 = pick1 + jnp.where(before == 1, flags[l], 0) * l
        before = before + flags[l]
    send_pick = jnp.where(grp == 0, pick1, pick0)
    own_pick = jnp.where(jnp.logical_and(grp == 1, count == 2), pick1, pick0)
    use_recv = count == 0

    row = lax.broadcasted_iota(jnp.int32, (HALF, HALF), 0)
    col = lax.broadcasted_iota(jnp.int32, (HALF, HALF), 1)
    lower_block = res[send_pick, HALF:, HALF:]
    pack[0:HALF] = res[send_pick, :HALF, HALF:]
    pack[HALF:2 * HALF] = jnp.where(row <= col, res[send_pick, :HALF, :HALF], lower_block)
    diagonal = jnp.sum(jnp.where(row == col, lower_block, 0.0), axis=0, keepdims=True)
    pack[2 * HALF:2 * HALF + 8] = jnp.broadcast_to(diagonal, (8, HALF))
    exchange = copy(pack, pack_recv, zs[3])
    exchange.start()

    def root_start():
        exchange.wait_recv()
        eye = (row == col).astype(F32)
        upper = pack_recv[HALF:2 * HALF]
        flipped = upper.T
        off = pack_recv[0:HALF]
        block_a = jnp.where(row <= col, upper, flipped)
        block_d = jnp.where(row > col, upper, flipped)
        block_d = jnp.where(row == col, jnp.broadcast_to(pack_recv[2 * HALF:2 * HALF + 1], (HALF, HALF)), block_d)
        total = jnp.zeros((1, 1), F32)
        for i, j, got in ((0, 0, block_a), (0, 1, off), (1, 0, off.T), (1, 1, block_d)):
            rows, cols = pl.ds(i * HALF, HALF), pl.ds(j * HALF, HALF)
            value = jnp.where(use_recv, got, res[own_pick, rows, cols])
            if i == j:
                value = value + EPSILON * eye
            m0[rows, cols] = value
            total = total + jnp.sum(value * value, axis=(0, 1), keepdims=True)
        zeta = 2.5 / jnp.sqrt(total + 1e-06)
        scale.append(jnp.sqrt(jnp.sqrt(zeta)))
        value = m0[...] * zeta
        m0[...] = value
        put(m0_h, m0_l, slice(None), value)

    scale = []

    def put(high, low, rows, value):
        value_h, value_l = split(value)
        high[rows, :] = value_h
        low[rows, :] = value_l

    def product(ah, al, bh, bl, rows):
        lead = ah[rows, :]
        return dot(lead, bh[...]) + dot(lead, bl[...]) + dot(al[rows, :], bh[...])

    def ident(i):
        r_ = lax.broadcasted_iota(jnp.int32, (ROWS, BLK), 0) + i * ROWS
        c_ = lax.broadcasted_iota(jnp.int32, (ROWS, BLK), 1)
        return (r_ == c_).astype(F32)

    def step1(i, rows):
        square = product(m0_h, m0_l, m0_h, m0_l, rows)
        m = m0[rows, :]
        put(w_h, w_l, rows, (5.0 * m - square) * 0.25)
        put(q_h, q_l, rows, (25.0 * ident(i) - 10.0 * m + square) * 0.0625)

    def step2(i, rows):
        put(r_h, r_l, rows, product(q_h, q_l, q_h, q_l, rows))

    def step3(i, rows):
        fifth = product(r_h, r_l, w_h, w_l, rows)
        factor = (5.0 * ident(i) - m0[rows, :]) * 0.25
        value = (5.0 * factor - fifth) * 0.25
        p_f[rows, :] = value
        put(p_h, p_l, rows, value)

    def step4(i, rows):
        put(q_h, q_l, rows, product(p_h, p_l, p_h, p_l, rows))

    def step5(i, rows):
        put(w_h, w_l, rows, product(p_h, p_l, m0_h, m0_l, rows))

    def step6(i, rows):
        fifth = product(r_h, r_l, w_h, w_l, rows)
        root_out[0, rows, :] = (5.0 * p_f[rows, :] - fifth) * (0.25 * scale[0])

    def root_steps():
        yield root_start()
        for body in (step1, step2, step3, step4, step5, step2, step6):
            for i in range(BLK // ROWS):
                yield body(i, pl.ds(i * ROWS, ROWS))

    steps = root_steps()

    def run(number):
        for _ in range(number):
            next(steps, None)

    phase1, phase2, phase3 = {}, {}, []
    for i, j in chunks:
        at = pl.ds(planes(i, j), PC)
        part = grad_part(i, j, c)
        core[i, j].wait_recv()
        g_own[at] = part + core_recv[at]
        here = pl.ds(j * PC, PC)
        group = []
        for k in range(1, 4):
            if i == 0:
                item = copy(g_own.at[at, :, (x + k) % NX], p1a.at[k - 1, here], xs[k - 1])
            else:
                item = copy(g_own.at[at, (y + k) % NY], p1b.at[k - 1, here], ys[k - 1])
            item.start()
            group.append(item)
        phase1[i, j] = group

    def second(i, j):
        here = pl.ds(j * PC, PC)
        at = pl.ds(planes(i, j), PC)
        for item in phase1[i, j]:
            item.wait_recv()
        got, total = (p1a, a1) if i == 0 else (p1b, b1)
        mine = g_own[at, :, x] if i == 0 else g_own[at, y]
        total[here] = mine + got[0, here] + got[1, here] + got[2, here]
        group = []
        for k in range(1, 4):
            if i == 0:
                item = copy(total.at[here, (y + k) % NY], p2a.at[k - 1, here], ys[k - 1])
            else:
                item = copy(total.at[here, (x + k) % NX], p2b.at[k - 1, here], xs[k - 1])
            item.start()
            group.append(item)
        phase2[i, j] = group

    z_base = [next(recvs) for _ in range(NZ)][0]

    def third(i, j):
        here = pl.ds(j * PC, PC)
        for item in phase2[i, j]:
            item.wait_recv()
        got, total, at = (p2a, a1, y) if i == 0 else (p2b, b1, x)
        r[pl.ds(planes(i, j), PC)] = total[here, at] + got[0, here] + got[1, here] + got[2, here]
        for q in range(PC):
            p = planes(i, j) + q
            item = copy(r.at[p], p3.at[z], dev(jnp.int32(p), y, x, c), recv_sem.at[z_base + z])
            pl.when(z != p)(item.start)
            phase3.append((z != p, item))

    for n, (i, j) in enumerate(chunks):
        second(i, j)
        if n >= LAG:
            third(*chunks[n - LAG])
    for n in range(len(chunks) - LAG, len(chunks)):
        third(*chunks[n])

    run(HOOKS[0])
    mine = r[z]
    for k in range(1, NZ):
        source = (z + k) % NZ
        pltpu.make_async_remote_copy(
            src_ref=r.at[z], dst_ref=p3.at[source], send_sem=send_sem.at[0],
            recv_sem=recv_sem.at[z_base + source], device_id=partner, device_id_type=MESH,
        ).wait_recv()
        mine = mine + p3[source]
    fin[...] = mine

    gz_base = [next(recvs) for _ in range(2)][0]
    near = c == zl // 2
    gz = []
    for t in range(2):
        to = 2 * c + t
        item = copy(
            fin, tile.at[zl, y, x], dev(grp * ZL + to, y, x, zl // 2), recv_sem.at[gz_base + zl % 2]
        )
        sent = jnp.logical_not(jnp.logical_and(near, to == zl))
        pl.when(sent)(item.start)
        gz.append((sent, item))
    swap = copy(fin, fin_other, partner)
    swap.start()

    run(HOOKS[1])

    def keep():
        tile[zl, y, x] = mine

    pl.when(near)(keep)
    for t in range(2):
        source = 2 * c + t
        item = pltpu.make_async_remote_copy(
            src_ref=fin, dst_ref=tile.at[source, y, x], send_sem=send_sem.at[0],
            recv_sem=recv_sem.at[gz_base + t], device_id=partner, device_id_type=MESH,
        )
        pl.when(jnp.logical_not(jnp.logical_and(near, source == zl)))(item.wait_recv)

    first, later, forward = [], [], []
    for side in range(2):
        two = pl.ds(2 * side, 2)
        one_peers, two_peers = (ys, xs) if side == 0 else (xs, ys)
        slabs = [
            tile.at[two, :, (x + 4 - k) % NX] if side == 0 else tile.at[two, (y + 4 - k) % NY]
            for k in range(4)
        ]
        spot = tile.at[two, y, x]
        if side == 0:
            ids = [(next(sends), next(recvs)) for _ in range(10)]

        def make(src, to, n):
            return pltpu.make_async_remote_copy(
                src_ref=src, dst_ref=src, send_sem=send_sem.at[ids[n][0]], recv_sem=recv_sem.at[ids[n][1]],
                device_id=to, device_id_type=MESH,
            )

        first.append([make(spot, one_peers[k], k) for k in range(3)])
        later.append([make(slabs[0], two_peers[k], 3 + k) for k in range(3)])
        forward.append([make(slabs[k], partner, 6 + k) for k in range(4)])

    def both(body):
        pl.when(c == 0)(lambda: body(0))
        pl.when(c == 1)(lambda: body(1))

    def gather_first(side):
        for item in first[side]:
            item.start()

    def gather_later(side):
        for item in first[side]:
            item.wait_recv()
        for item in later[side]:
            item.start()
        forward[side][0].start()

    def gather_end(side):
        for k in range(1, 4):
            later[side][k - 1].wait_recv()
            forward[side][k].start()

    def gather_take(side):
        for k in range(4):
            forward[1 - side][k].wait_recv()

    both(gather_first)
    run(HOOKS[2])
    both(gather_later)
    run(HOOKS[3])
    both(gather_end)
    run(HOOKS[4])

    swap.wait_recv()
    low = jnp.where(c == 0, fin[...], fin_other[...])
    high = jnp.where(c == 0, fin_other[...], fin[...])
    grad_out[:, :BLK] = jnp.where(c == 0, low[:4], low[4:])
    grad_out[:, BLK:] = jnp.where(c == 0, high[:4], high[4:])
    both(gather_take)

    t_value = tile[...].reshape(BLK, BLK)
    t_h, t_l = split(t_value)
    t_high[...] = t_h
    t_low[...] = t_l
    at = (f % 32) * 16

    def left():
        dims = (((1,), (1,)), ((), ()))
        rows = pl.ds(pl.multiple_of(at, 16), 16)
        lead_h, lead_l = t_high[rows, :], t_low[rows, :]
        part = dot(lead_h, t_high[...], dims) + dot(lead_h, t_low[...], dims) + dot(lead_l, t_high[...], dims)
        stats_out[...] = stats_in[...] + part * (1.0 / BLK)

    def right():
        dims = (((0,), (0,)), ((), ()))
        columns = pl.ds(pl.multiple_of(at // 128 * 128, 128), 128)
        lead_h, lead_l = t_high[:, columns], t_low[:, columns]
        wide[...] = dot(lead_h, t_high[...], dims) + dot(lead_h, t_low[...], dims) + dot(lead_l, t_high[...], dims)
        part = wide[pl.ds(pl.multiple_of(at % 128, 16), 16), :]
        stats_out[...] = stats_in[...] + part * (1.0 / BLK)

    pl.when(zl % 2 == 0)(left)
    pl.when(zl % 2 == 1)(right)
    run(20)

    for group in [list(core.values()), [exchange, swap]] + list(phase1.values()) + list(phase2.values()):
        for item in group:
            item.wait_send()
    for sent, item in phase3 + gz:
        pl.when(sent)(item.wait_send)

    def sent_all(side):
        for item in first[side] + later[side] + forward[side]:
            item.wait_send()

    both(sent_all)


def on_device(hidden_act, out_grad, layer_stats, resident_stats, slot_block, layer_refresh):
    vmem = pl.BlockSpec(memory_space=pltpu.VMEM)
    hbm = pl.BlockSpec(memory_space=pltpu.HBM)
    square = (BLK, BLK)
    piece = (8, BLK)
    scratch = [
        pltpu.VMEM(hidden_act.shape, BF16),
        pltpu.VMEM(out_grad.shape, BF16),
        pltpu.VMEM(layer_stats.shape, F32),
        pltpu.VMEM(resident_stats.shape, F32),
        pltpu.SMEM(slot_block.shape, jnp.int32),
        pltpu.SMEM(layer_refresh.shape, jnp.int32),
        pltpu.VMEM((NZ, NY, NX) + piece, F32),
        pltpu.VMEM((NZ, NY, NX) + piece, F32),
        pltpu.VMEM((NZ, NY, NX) + piece, F32),
        pltpu.VMEM((3, 4, NY) + piece, F32),
        pltpu.VMEM((3, 4, NX) + piece, F32),
        pltpu.VMEM((4, NY) + piece, F32),
        pltpu.VMEM((4, NX) + piece, F32),
        pltpu.VMEM((3, 4) + piece, F32),
        pltpu.VMEM((3, 4) + piece, F32),
        pltpu.VMEM((NZ,) + piece, F32),
        pltpu.VMEM((NZ,) + piece, F32),
        pltpu.VMEM(piece, F32),
        pltpu.VMEM(piece, F32),
        pltpu.VMEM((ZL, NY, NX) + piece, F32),
        pltpu.VMEM(square, BF16),
        pltpu.VMEM(square, BF16),
        pltpu.VMEM((128, BLK), F32),
        pltpu.VMEM((2 * HALF + 8, HALF), F32),
        pltpu.VMEM((2 * HALF + 8, HALF), F32),
        pltpu.VMEM(square, F32),
        pltpu.VMEM(square, BF16),
        pltpu.VMEM(square, BF16),
        pltpu.VMEM(square, BF16),
        pltpu.VMEM(square, BF16),
        pltpu.VMEM(square, BF16),
        pltpu.VMEM(square, BF16),
        pltpu.VMEM(square, BF16),
        pltpu.VMEM(square, BF16),
        pltpu.VMEM(square, F32),
        pltpu.VMEM(square, BF16),
        pltpu.VMEM(square, BF16),
        pltpu.SemaphoreType.DMA((6,)),
        pltpu.SemaphoreType.DMA((SEMS,)),
        pltpu.SemaphoreType.DMA((SEMS,)),
    ]
    return pl.pallas_call(
        kernel,
        out_shape=(
            jax.ShapeDtypeStruct((4, 1024), F32),
            jax.ShapeDtypeStruct(layer_stats.shape, F32),
            jax.ShapeDtypeStruct((1, BLK, BLK), F32),
        ),
        in_specs=[hbm] * 6,
        out_specs=(vmem, vmem, vmem),
        scratch_shapes=scratch,
        compiler_params=pltpu.CompilerParams(
            collective_id=0, has_side_effects=True, vmem_limit_bytes=48 * 1024 * 1024
        ),
        cost_estimate=pl.CostEstimate(flops=10**10, bytes_accessed=10**7, transcendentals=0),
    )(hidden_act, out_grad, layer_stats, resident_stats, slot_block, layer_refresh)


def solution(mesh):
    in_specs = (
        P(("grp", "fsdp"), None),
        P(("grp", "fsdp"), None),
        P(("grp", "fsdp"), None),
        P(("grp", "fsdp"), None, None),
        P(),
        P(),
    )
    out_specs = (P(("grp", "fsdp"), None), P(("grp", "fsdp"), None), P(("grp", "fsdp"), None, None))
    return jax.shard_map(
        on_device, mesh=mesh, in_specs=in_specs, out_specs=out_specs, check_vma=False
    )
```

```python
import jax
import jax.numpy as jnp
from jax import lax
from jax.experimental import pallas as pl
from jax.experimental.pallas import tpu as pltpu
from jax.sharding import PartitionSpec as P

BPL = 16
EPSILON = 0.0001
MESH = pl.DeviceIdType.MESH
F32 = jnp.float32
BF16 = jnp.bfloat16
ZL, NY, NX, NZ = 4, 4, 4, 8
BLK = 512
HALF = 256
ROWS = 256
NCH = 2
PC = 4 // NCH
LAG = 2
HOOKS = (0, 8, 7, 0)
SEMS = 100


def split(value):
    high = value.astype(BF16)
    return high, (value - high.astype(F32)).astype(BF16)


def dot(a, b, dims=(((1,), (0,)), ((), ()))):
    return lax.dot_general(a, b, dims, preferred_element_type=F32)


def kernel(
    hid_any, og_any, stats_any, res_any, slots_any, refresh_any,
    grad_out, stats_out, root_out,
    hid, og, stats_in, res, slot_block, refresh,
    g_send, g_own, core_recv, s1a, s1b, p1a, p1b, a1, b1, p2a, p2b, r, p3, fin, fin_other,
    tile, t_high, t_low, wide, pack, pack_recv,
    m0, m0_h, m0_l, q_h, q_l, r_h, r_l, w_h, w_l, p_f, p_h, p_l,
    in_sem, send_sem, recv_sem,
):
    grp = lax.axis_index("grp")
    f = lax.axis_index("fsdp")
    zl = f // 32
    y = (f // 8) % NY
    x = (f // 2) % NX
    c = f % 2
    z = grp * ZL + zl

    def dev(z_, y_, x_, c_):
        return (z_ // ZL, (z_ % ZL) * 32 + y_ * 8 + x_ * 2 + c_)

    partner = dev(z, y, x, 1 - c)
    xs = [dev(z, y, (x + k) % NX, c) for k in range(1, NX)]
    ys = [dev(z, (y + k) % NY, x, c) for k in range(1, NY)]
    zs = [dev((z + k) % NZ, y, x, c) for k in range(1, NZ)]

    sends = iter(range(SEMS))
    recvs = iter(range(SEMS))

    def copy(src, dst, to, recv=None):
        return pltpu.make_async_remote_copy(
            src_ref=src, dst_ref=dst, send_sem=send_sem.at[next(sends)],
            recv_sem=recv_sem.at[next(recvs)] if recv is None else recv,
            device_id=to, device_id_type=MESH,
        )

    keeper = zl // 2

    def gather_to(t, k):
        to_y = jnp.where(keeper == 0, (y + k) % NY, y)
        to_x = jnp.where(keeper == 0, x, (x + k) % NX)
        return dev(grp * ZL + 2 * c + t, to_y, to_x, keeper)

    def gather_from(t, k):
        from_y = jnp.where(c == 0, (y + 4 - k) % NY, y)
        from_x = jnp.where(c == 0, x, (x + 4 - k) % NX)
        return dev(grp * ZL + 2 * c + t, from_y, from_x, keeper)

    barrier = pltpu.get_barrier_semaphore()
    peers = [partner] + xs + ys + zs
    cross = [dev(grp * ZL + (zl + k) % ZL, y, x, 1 - c) for k in range(1, ZL)]
    peers = peers + cross
    for t in range(2):
        for k in range(1, 4):
            peers.append(gather_to(t, k))
            peers.append(gather_from(t, k))
    for peer in peers:
        pl.semaphore_signal(barrier, inc=1, device_id=peer, device_id_type=MESH)
    loads = [
        pltpu.make_async_copy(src, dst, in_sem.at[i])
        for i, (src, dst) in enumerate([
            (slots_any, slot_block), (refresh_any, refresh), (og_any, og), (hid_any, hid),
            (res_any, res), (stats_any, stats_in),
        ])
    ]
    for load in loads:
        load.start()

    def planes(i, j):
        return 4 * i + j * PC

    def grad_part(i, j, half):
        rows = pl.ds(planes(i, j) * 128, PC * 128)
        columns = pl.ds(pl.multiple_of(half * BLK, BLK), BLK)
        part = dot(hid[:, rows], og[:, columns], (((0,), (0,)), ((), ())))
        return part.reshape(PC, NY, NX, 8, BLK)

    chunks = [(i, j) for j in range(NCH) for i in range(2)]

    loads[0].wait()
    loads[1].wait()
    own = (grp * 128 + f) * 4
    flags = [refresh[slot_block[own + l] // BPL] for l in range(4)]
    count = flags[0] + flags[1] + flags[2] + flags[3]
    pick0 = jnp.int32(0)
    pick1 = jnp.int32(0)
    before = jnp.int32(0)
    for l in range(4):
        pick0 = pick0 + jnp.where(before == 0, flags[l], 0) * l
        pick1 = pick1 + jnp.where(before == 1, flags[l], 0) * l
        before = before + flags[l]
    send_pick = jnp.where(grp == 0, pick1, pick0)
    own_pick = jnp.where(jnp.logical_and(grp == 1, count == 2), pick1, pick0)
    use_recv = count == 0

    loads[2].wait()
    loads[3].wait()
    core = {}
    for i, j in chunks:
        at = pl.ds(planes(i, j), PC)
        g_send[at] = grad_part(i, j, 1 - c)
        core[i, j] = copy(g_send.at[at], core_recv.at[at], partner)

    row = lax.broadcasted_iota(jnp.int32, (HALF, HALF), 0)
    col = lax.broadcasted_iota(jnp.int32, (HALF, HALF), 1)
    loads[4].wait()
    loads[5].wait()
    lower_block = res[send_pick, HALF:, HALF:]
    pack[0:HALF] = res[send_pick, :HALF, HALF:]
    pack[HALF:2 * HALF] = jnp.where(row <= col, res[send_pick, :HALF, :HALF], lower_block)
    diagonal = jnp.sum(jnp.where(row == col, lower_block, 0.0), axis=0, keepdims=True)
    pack[2 * HALF:2 * HALF + 8] = jnp.broadcast_to(diagonal, (8, HALF))
    exchange = copy(pack, pack_recv, zs[3])

    pl.semaphore_wait(barrier, len(peers))
    core[0, 0].start()
    exchange.start()
    for item in chunks[1:]:
        core[item].start()

    def root_start():
        exchange.wait_recv()
        eye = (row == col).astype(F32)
        upper = pack_recv[HALF:2 * HALF]
        flipped = upper.T
        off = pack_recv[0:HALF]
        block_a = jnp.where(row <= col, upper, flipped)
        block_d = jnp.where(row > col, upper, flipped)
        block_d = jnp.where(row == col, jnp.broadcast_to(pack_recv[2 * HALF:2 * HALF + 1], (HALF, HALF)), block_d)
        total = jnp.zeros((1, 1), F32)
        for i, j, got in ((0, 0, block_a), (0, 1, off), (1, 0, off.T), (1, 1, block_d)):
            rows, cols = pl.ds(i * HALF, HALF), pl.ds(j * HALF, HALF)
            value = jnp.where(use_recv, got, res[own_pick, rows, cols])
            if i == j:
                value = value + EPSILON * eye
            m0[rows, cols] = value
            total = total + jnp.sum(value * value, axis=(0, 1), keepdims=True)
        zeta = 2.5 / jnp.sqrt(total + 1e-06)
        scale.append(jnp.sqrt(jnp.sqrt(zeta)))
        value = m0[...] * zeta
        m0[...] = value
        put(m0_h, m0_l, slice(None), value)

    scale = []

    def put(high, low, rows, value):
        value_h, value_l = split(value)
        high[rows, :] = value_h
        low[rows, :] = value_l

    def product(ah, al, bh, bl, rows):
        lead = ah[rows, :]
        return dot(lead, bh[...]) + dot(lead, bl[...]) + dot(al[rows, :], bh[...])

    def ident(i):
        r_ = lax.broadcasted_iota(jnp.int32, (ROWS, BLK), 0) + i * ROWS
        c_ = lax.broadcasted_iota(jnp.int32, (ROWS, BLK), 1)
        return (r_ == c_).astype(F32)

    def step1(i, rows):
        square = product(m0_h, m0_l, m0_h, m0_l, rows)
        m = m0[rows, :]
        put(w_h, w_l, rows, (5.0 * m - square) * 0.25)
        put(q_h, q_l, rows, (25.0 * ident(i) - 10.0 * m + square) * 0.0625)

    def step2(i, rows):
        put(r_h, r_l, rows, product(q_h, q_l, q_h, q_l, rows))

    def step3(i, rows):
        fifth = product(r_h, r_l, w_h, w_l, rows)
        factor = (5.0 * ident(i) - m0[rows, :]) * 0.25
        value = (5.0 * factor - fifth) * 0.25
        p_f[rows, :] = value
        put(p_h, p_l, rows, value)

    def step4(i, rows):
        put(q_h, q_l, rows, product(p_h, p_l, p_h, p_l, rows))

    def step5(i, rows):
        put(w_h, w_l, rows, product(p_h, p_l, m0_h, m0_l, rows))

    def step6(i, rows):
        fifth = product(r_h, r_l, w_h, w_l, rows)
        root_out[0, rows, :] = (5.0 * p_f[rows, :] - fifth) * (0.25 * scale[0])

    def root_steps():
        yield root_start()
        for body in (step1, step2, step3, step4, step5, step2, step6):
            for i in range(BLK // ROWS):
                yield body(i, pl.ds(i * ROWS, ROWS))

    steps = root_steps()

    def run(number):
        for _ in range(number):
            next(steps, None)

    met, phase1, phase2, phase3 = {}, {}, {}, []
    half_recv, whole_recv = (s1a, s1b), (p1a, p1b)

    def axis(i):
        return (xs[0], xs[2]) if i == 0 else (ys[0], ys[2])

    def spot(i, plane, k):
        return g_own.at[plane, :, (x + k) % NX] if i == 0 else g_own.at[plane, (y + k) % NY]

    for i, j in chunks:
        at = pl.ds(planes(i, j), PC)
        part = grad_part(i, j, c)
        core[i, j].wait_recv()
        g_own[at] = part + core_recv[at]
        low, high = planes(i, j), planes(i, j) + 1
        plus, minus = axis(i)
        met[i, j] = [
            copy(spot(i, low, 2), half_recv[i].at[0, j], plus),
            copy(spot(i, high, 2), half_recv[i].at[1, j], minus),
        ]
        phase1[i, j] = [
            copy(spot(i, high, 1), whole_recv[i].at[0, 2 * j + 1], plus),
            copy(spot(i, low, 3), whole_recv[i].at[1, 2 * j], minus),
        ]
        for item in met[i, j] + phase1[i, j]:
            item.start()
    for i, j in chunks:
        low, high = planes(i, j), planes(i, j) + 1
        plus, minus = axis(i)
        for side, (plane, k, to) in enumerate(((low, 1, plus), (high, 3, minus))):
            met[i, j][side].wait_recv()
            there = spot(i, plane, k)
            there[...] = there[...] + half_recv[i][side, j]
            item = copy(there, whole_recv[i].at[side, 2 * j + side], to)
            item.start()
            phase1[i, j].append(item)

    def second(i, j):
        here = pl.ds(j * PC, PC)
        at = pl.ds(planes(i, j), PC)
        for item in phase1[i, j]:
            item.wait_recv()
        got, total = whole_recv[i], (a1, b1)[i]
        mine = g_own[at, :, x] if i == 0 else g_own[at, y]
        total[here] = mine + got[0, here] + got[1, here]
        group = []
        for k in range(1, 4):
            if i == 0:
                item = copy(total.at[here, (y + k) % NY], p2a.at[k - 1, here], ys[k - 1])
            else:
                item = copy(total.at[here, (x + k) % NX], p2b.at[k - 1, here], xs[k - 1])
            item.start()
            group.append(item)
        phase2[i, j] = group

    z_base = [next(recvs) for _ in range(NZ)][0]

    def third(i, j):
        here = pl.ds(j * PC, PC)
        for item in phase2[i, j]:
            item.wait_recv()
        got, total, at = (p2a, a1, y) if i == 0 else (p2b, b1, x)
        r[pl.ds(planes(i, j), PC)] = total[here, at] + got[0, here] + got[1, here] + got[2, here]
        for q in range(PC):
            p = planes(i, j) + q
            item = copy(r.at[p], p3.at[z], dev(jnp.int32(p), y, x, c), recv_sem.at[z_base + z])
            pl.when(z != p)(item.start)
            phase3.append((z != p, item))

    for n, (i, j) in enumerate(chunks):
        second(i, j)
        if n >= LAG:
            third(*chunks[n - LAG])
    for n in range(len(chunks) - LAG, len(chunks)):
        third(*chunks[n])

    run(HOOKS[0])
    mine = r[z]
    for k in range(1, NZ):
        source = (z + k) % NZ
        pltpu.make_async_remote_copy(
            src_ref=r.at[z], dst_ref=p3.at[source], send_sem=send_sem.at[0],
            recv_sem=recv_sem.at[z_base + source], device_id=partner, device_id_type=MESH,
        ).wait_recv()
        mine = mine + p3[source]
    fin[...] = mine

    gz_base = [next(recvs) for _ in range(8)][0]
    near = c == keeper
    gz = []
    for k in range(4):
        for t in range(2):
            item = copy(
                fin, tile.at[zl, y, x], gather_to(t, k), recv_sem.at[gz_base + 4 * (zl % 2) + k]
            )
            if k == 0:
                sent = jnp.logical_not(jnp.logical_and(near, 2 * c + t == zl))
                pl.when(sent)(item.start)
                gz.append((sent, item))
            else:
                item.start()
                gz.append((None, item))
    swap = copy(fin, fin_other, partner)
    swap.start()

    def keep():
        tile[zl, y, x] = mine

    pl.when(near)(keep)
    run(HOOKS[1])
    for k in range(4):
        for t in range(2):
            source = 2 * c + t
            from_y = jnp.where(c == 0, (y + 4 - k) % NY, y)
            from_x = jnp.where(c == 0, x, (x + 4 - k) % NX)
            item = pltpu.make_async_remote_copy(
                src_ref=fin, dst_ref=tile.at[source, from_y, from_x], send_sem=send_sem.at[0],
                recv_sem=recv_sem.at[gz_base + 4 * t + k], device_id=partner, device_id_type=MESH,
            )
            if k == 0:
                pl.when(jnp.logical_not(jnp.logical_and(near, source == zl)))(item.wait_recv)
            else:
                item.wait_recv()

    ids = [(next(sends), next(recvs)) for _ in range(7)]
    later, forward = [], []
    for side in range(2):
        two = pl.ds(2 * side, 2)
        slabs = [
            tile.at[two, :, (x + 4 - k) % NX] if side == 0 else tile.at[two, (y + 4 - k) % NY]
            for k in range(4)
        ]

        def make(src, to, n):
            return pltpu.make_async_remote_copy(
                src_ref=src, dst_ref=src, send_sem=send_sem.at[ids[n][0]], recv_sem=recv_sem.at[ids[n][1]],
                device_id=to, device_id_type=MESH,
            )

        later.append([make(slabs[0], (xs, ys)[side][k], k) for k in range(3)])
        forward.append([make(slabs[k], partner, 3 + k) for k in range(4)])

    def both(body):
        pl.when(c == 0)(lambda: body(0))
        pl.when(c == 1)(lambda: body(1))

    def gather_later(side):
        for item in later[side]:
            item.start()
        forward[side][0].start()

    def gather_end(side):
        for k in (1, 3, 2):
            later[side][k - 1].wait_recv()
            forward[side][k].start()

    def gather_take(side):
        for k in (0, 1, 3, 2):
            forward[1 - side][k].wait_recv()

    both(gather_later)
    run(HOOKS[2])
    both(gather_end)
    run(HOOKS[3])

    swap.wait_recv()
    low = jnp.where(c == 0, fin[...], fin_other[...])
    high = jnp.where(c == 0, fin_other[...], fin[...])
    grad_out[:, :BLK] = jnp.where(c == 0, low[:4], low[4:])
    grad_out[:, BLK:] = jnp.where(c == 0, high[:4], high[4:])
    both(gather_take)

    t_value = tile[...].reshape(BLK, BLK)
    t_h, t_l = split(t_value)
    t_high[...] = t_h
    t_low[...] = t_l
    at = (f % 32) * 16

    def left():
        dims = (((1,), (1,)), ((), ()))
        rows = pl.ds(pl.multiple_of(at, 16), 16)
        lead_h, lead_l = t_high[rows, :], t_low[rows, :]
        part = dot(lead_h, t_high[...], dims) + dot(lead_h, t_low[...], dims) + dot(lead_l, t_high[...], dims)
        stats_out[...] = stats_in[...] + part * (1.0 / BLK)

    def right():
        dims = (((0,), (0,)), ((), ()))
        columns = pl.ds(pl.multiple_of(at // 128 * 128, 128), 128)
        lead_h, lead_l = t_high[:, columns], t_low[:, columns]
        wide[...] = dot(lead_h, t_high[...], dims) + dot(lead_h, t_low[...], dims) + dot(lead_l, t_high[...], dims)
        part = wide[pl.ds(pl.multiple_of(at % 128, 16), 16), :]
        stats_out[...] = stats_in[...] + part * (1.0 / BLK)

    pl.when(zl % 2 == 0)(left)
    pl.when(zl % 2 == 1)(right)
    run(20)

    for group in [list(core.values()), [exchange, swap]] + list(met.values()) + list(phase1.values()) + list(phase2.values()):
        for item in group:
            item.wait_send()
    for sent, item in phase3 + gz:
        if sent is None:
            item.wait_send()
        else:
            pl.when(sent)(item.wait_send)

    def sent_all(side):
        for item in later[side] + forward[side]:
            item.wait_send()

    both(sent_all)


def on_device(hidden_act, out_grad, layer_stats, resident_stats, slot_block, layer_refresh):
    vmem = pl.BlockSpec(memory_space=pltpu.VMEM)
    hbm = pl.BlockSpec(memory_space=pltpu.HBM)
    square = (BLK, BLK)
    piece = (8, BLK)
    scratch = [
        pltpu.VMEM(hidden_act.shape, BF16),
        pltpu.VMEM(out_grad.shape, BF16),
        pltpu.VMEM(layer_stats.shape, F32),
        pltpu.VMEM(resident_stats.shape, F32),
        pltpu.SMEM(slot_block.shape, jnp.int32),
        pltpu.SMEM(layer_refresh.shape, jnp.int32),
        pltpu.VMEM((NZ, NY, NX) + piece, F32),
        pltpu.VMEM((NZ, NY, NX) + piece, F32),
        pltpu.VMEM((NZ, NY, NX) + piece, F32),
        pltpu.VMEM((2, 2, NY) + piece, F32),
        pltpu.VMEM((2, 2, NX) + piece, F32),
        pltpu.VMEM((2, 4, NY) + piece, F32),
        pltpu.VMEM((2, 4, NX) + piece, F32),
        pltpu.VMEM((4, NY) + piece, F32),
        pltpu.VMEM((4, NX) + piece, F32),
        pltpu.VMEM((3, 4) + piece, F32),
        pltpu.VMEM((3, 4) + piece, F32),
        pltpu.VMEM((NZ,) + piece, F32),
        pltpu.VMEM((NZ,) + piece, F32),
        pltpu.VMEM(piece, F32),
        pltpu.VMEM(piece, F32),
        pltpu.VMEM((ZL, NY, NX) + piece, F32),
        pltpu.VMEM(square, BF16),
        pltpu.VMEM(square, BF16),
        pltpu.VMEM((128, BLK), F32),
        pltpu.VMEM((2 * HALF + 8, HALF), F32),
        pltpu.VMEM((2 * HALF + 8, HALF), F32),
        pltpu.VMEM(square, F32),
        pltpu.VMEM(square, BF16),
        pltpu.VMEM(square, BF16),
        pltpu.VMEM(square, BF16),
        pltpu.VMEM(square, BF16),
        pltpu.VMEM(square, BF16),
        pltpu.VMEM(square, BF16),
        pltpu.VMEM(square, BF16),
        pltpu.VMEM(square, BF16),
        pltpu.VMEM(square, F32),
        pltpu.VMEM(square, BF16),
        pltpu.VMEM(square, BF16),
        pltpu.SemaphoreType.DMA((6,)),
        pltpu.SemaphoreType.DMA((SEMS,)),
        pltpu.SemaphoreType.DMA((SEMS,)),
    ]
    return pl.pallas_call(
        kernel,
        out_shape=(
            jax.ShapeDtypeStruct((4, 1024), F32),
            jax.ShapeDtypeStruct(layer_stats.shape, F32),
            jax.ShapeDtypeStruct((1, BLK, BLK), F32),
        ),
        in_specs=[hbm] * 6,
        out_specs=(vmem, vmem, vmem),
        scratch_shapes=scratch,
        compiler_params=pltpu.CompilerParams(
            collective_id=0, has_side_effects=True, vmem_limit_bytes=48 * 1024 * 1024
        ),
        cost_estimate=pl.CostEstimate(flops=10**10, bytes_accessed=10**7, transcendentals=0),
    )(*[
        pltpu.with_memory_space_constraint(value, pltpu.HBM)
        for value in (hidden_act, out_grad, layer_stats, resident_stats, slot_block, layer_refresh)
    ])


def solution(mesh):
    in_specs = (
        P(("grp", "fsdp"), None),
        P(("grp", "fsdp"), None),
        P(("grp", "fsdp"), None),
        P(("grp", "fsdp"), None, None),
        P(),
        P(),
    )
    out_specs = (P(("grp", "fsdp"), None), P(("grp", "fsdp"), None), P(("grp", "fsdp"), None, None))
    return jax.shard_map(
        on_device, mesh=mesh, in_specs=in_specs, out_specs=out_specs, check_vma=False
    )
```

```python
import jax
import jax.numpy as jnp
from jax import lax
from jax.experimental import pallas as pl
from jax.experimental.pallas import tpu as pltpu
from jax.sharding import PartitionSpec as P

BPL = 16
EPSILON = 0.0001
MESH = pl.DeviceIdType.MESH
F32 = jnp.float32
BF16 = jnp.bfloat16
ZL, NY, NX, NZ = 4, 4, 4, 8
BLK = 512
HALF = 256
ROWS = 256
NCH = 2
PC = 4 // NCH
LAG = 2
HOOKS = (0, 8, 7, 0)
SEMS = 100
CUTS = (400, 408)


def split(value):
    high = value.astype(BF16)
    return high, (value - high.astype(F32)).astype(BF16)


def dot(a, b, dims=(((1,), (0,)), ((), ()))):
    return lax.dot_general(a, b, dims, preferred_element_type=F32)


def kernel(
    hid_any, og_any, stats_any, res_any, slots_any, refresh_any,
    grad_out, stats_out, root_out,
    hid, og, stats_in, res, slot_block, refresh,
    g_send, g_own, core_recv, s1a, s1b, p1a, p1b, a1, b1, p2a, p2b, r, p3, fin, fin_other,
    tile, t_high, t_low, wide, pack, pack_recv,
    m0, m0_h, m0_l, q_h, q_l, r_h, r_l, w_h, w_l, p_f, p_h, p_l,
    in_sem, send_sem, recv_sem,
):
    grp = lax.axis_index("grp")
    f = lax.axis_index("fsdp")
    zl = f // 32
    y = (f // 8) % NY
    x = (f // 2) % NX
    c = f % 2
    z = grp * ZL + zl

    def dev(z_, y_, x_, c_):
        return (z_ // ZL, (z_ % ZL) * 32 + y_ * 8 + x_ * 2 + c_)

    partner = dev(z, y, x, 1 - c)
    xs = [dev(z, y, (x + k) % NX, c) for k in range(1, NX)]
    ys = [dev(z, (y + k) % NY, x, c) for k in range(1, NY)]
    zs = [dev((z + k) % NZ, y, x, c) for k in range(1, NZ)]

    sends = iter(range(SEMS))
    recvs = iter(range(SEMS))

    def copy(src, dst, to, recv=None):
        return pltpu.make_async_remote_copy(
            src_ref=src, dst_ref=dst, send_sem=send_sem.at[next(sends)],
            recv_sem=recv_sem.at[next(recvs)] if recv is None else recv,
            device_id=to, device_id_type=MESH,
        )

    keeper = zl // 2

    def gather_to(t, k):
        to_y = jnp.where(keeper == 0, (y + k) % NY, y)
        to_x = jnp.where(keeper == 0, x, (x + k) % NX)
        return dev(grp * ZL + 2 * c + t, to_y, to_x, keeper)

    def gather_from(t, k):
        from_y = jnp.where(c == 0, (y + 4 - k) % NY, y)
        from_x = jnp.where(c == 0, x, (x + 4 - k) % NX)
        return dev(grp * ZL + 2 * c + t, from_y, from_x, keeper)

    barrier = pltpu.get_barrier_semaphore()
    peers = [partner] + xs + ys + zs
    cross = [dev(grp * ZL + (zl + k) % ZL, y, x, 1 - c) for k in range(1, ZL)]
    peers = peers + cross
    for t in range(2):
        for k in range(1, 4):
            peers.append(gather_to(t, k))
            peers.append(gather_from(t, k))
    for peer in peers:
        pl.semaphore_signal(barrier, inc=1, device_id=peer, device_id_type=MESH)
    loads = [
        pltpu.make_async_copy(src, dst, in_sem.at[i])
        for i, (src, dst) in enumerate([
            (slots_any, slot_block), (refresh_any, refresh), (og_any, og), (hid_any, hid),
            (res_any, res), (stats_any, stats_in),
        ])
    ]
    for load in loads:
        load.start()

    def planes(i, j):
        return 4 * i + j * PC

    def grad_part(i, j, half):
        rows = pl.ds(planes(i, j) * 128, PC * 128)
        columns = pl.ds(pl.multiple_of(half * BLK, BLK), BLK)
        part = dot(hid[:, rows], og[:, columns], (((0,), (0,)), ((), ())))
        return part.reshape(PC, NY, NX, 8, BLK)

    chunks = [(i, j) for j in range(NCH) for i in range(2)]

    loads[0].wait()
    loads[1].wait()
    own = (grp * 128 + f) * 4
    flags = [refresh[slot_block[own + l] // BPL] for l in range(4)]
    count = flags[0] + flags[1] + flags[2] + flags[3]
    pick0 = jnp.int32(0)
    pick1 = jnp.int32(0)
    before = jnp.int32(0)
    for l in range(4):
        pick0 = pick0 + jnp.where(before == 0, flags[l], 0) * l
        pick1 = pick1 + jnp.where(before == 1, flags[l], 0) * l
        before = before + flags[l]
    send_pick = jnp.where(grp == 0, pick1, pick0)
    own_pick = jnp.where(jnp.logical_and(grp == 1, count == 2), pick1, pick0)
    use_recv = count == 0

    loads[2].wait()
    loads[3].wait()
    core = {}
    for i, j in chunks:
        at = pl.ds(planes(i, j), PC)
        g_send[at] = grad_part(i, j, 1 - c)
        core[i, j] = copy(g_send.at[at], core_recv.at[at], partner)

    row = lax.broadcasted_iota(jnp.int32, (HALF, HALF), 0)
    col = lax.broadcasted_iota(jnp.int32, (HALF, HALF), 1)
    loads[4].wait()
    loads[5].wait()
    lower_block = res[send_pick, HALF:, HALF:]
    pack[0:HALF] = res[send_pick, :HALF, HALF:]
    pack[HALF:2 * HALF] = jnp.where(row <= col, res[send_pick, :HALF, :HALF], lower_block)
    diagonal = jnp.sum(jnp.where(row == col, lower_block, 0.0), axis=0, keepdims=True)
    pack[2 * HALF:2 * HALF + 8] = jnp.broadcast_to(diagonal, (8, HALF))
    exchange = []
    for first, last in zip((0,) + CUTS, CUTS + (2 * HALF + 8,)):
        rows = pl.ds(first, last - first)
        exchange.append(copy(pack.at[rows], pack_recv.at[rows], zs[3]))

    pl.semaphore_wait(barrier, len(peers))
    core[0, 0].start()
    exchange[0].start()
    for item in chunks[1:]:
        core[item].start()

    def root_start():
        for item in exchange:
            item.wait_recv()
        eye = (row == col).astype(F32)
        upper = pack_recv[HALF:2 * HALF]
        flipped = upper.T
        off = pack_recv[0:HALF]
        block_a = jnp.where(row <= col, upper, flipped)
        block_d = jnp.where(row > col, upper, flipped)
        block_d = jnp.where(row == col, jnp.broadcast_to(pack_recv[2 * HALF:2 * HALF + 1], (HALF, HALF)), block_d)
        total = jnp.zeros((1, 1), F32)
        for i, j, got in ((0, 0, block_a), (0, 1, off), (1, 0, off.T), (1, 1, block_d)):
            rows, cols = pl.ds(i * HALF, HALF), pl.ds(j * HALF, HALF)
            value = jnp.where(use_recv, got, res[own_pick, rows, cols])
            if i == j:
                value = value + EPSILON * eye
            m0[rows, cols] = value
            total = total + jnp.sum(value * value, axis=(0, 1), keepdims=True)
        zeta = 2.5 / jnp.sqrt(total + 1e-06)
        scale.append(jnp.sqrt(jnp.sqrt(zeta)))
        value = m0[...] * zeta
        m0[...] = value
        put(m0_h, m0_l, slice(None), value)

    scale = []

    def put(high, low, rows, value):
        value_h, value_l = split(value)
        high[rows, :] = value_h
        low[rows, :] = value_l

    def product(ah, al, bh, bl, rows):
        lead = ah[rows, :]
        return dot(lead, bh[...]) + dot(lead, bl[...]) + dot(al[rows, :], bh[...])

    def ident(i):
        r_ = lax.broadcasted_iota(jnp.int32, (ROWS, BLK), 0) + i * ROWS
        c_ = lax.broadcasted_iota(jnp.int32, (ROWS, BLK), 1)
        return (r_ == c_).astype(F32)

    def step1(i, rows):
        square = product(m0_h, m0_l, m0_h, m0_l, rows)
        m = m0[rows, :]
        put(w_h, w_l, rows, (5.0 * m - square) * 0.25)
        put(q_h, q_l, rows, (25.0 * ident(i) - 10.0 * m + square) * 0.0625)

    def step2(i, rows):
        put(r_h, r_l, rows, product(q_h, q_l, q_h, q_l, rows))

    def step3(i, rows):
        fifth = product(r_h, r_l, w_h, w_l, rows)
        factor = (5.0 * ident(i) - m0[rows, :]) * 0.25
        value = (5.0 * factor - fifth) * 0.25
        p_f[rows, :] = value
        put(p_h, p_l, rows, value)

    def step4(i, rows):
        put(q_h, q_l, rows, product(p_h, p_l, p_h, p_l, rows))

    def step5(i, rows):
        put(w_h, w_l, rows, product(p_h, p_l, m0_h, m0_l, rows))

    def step6(i, rows):
        fifth = product(r_h, r_l, w_h, w_l, rows)
        root_out[0, rows, :] = (5.0 * p_f[rows, :] - fifth) * (0.25 * scale[0])

    def root_steps():
        yield root_start()
        for body in (step1, step2, step3, step4, step5, step2, step6):
            for i in range(BLK // ROWS):
                yield body(i, pl.ds(i * ROWS, ROWS))

    steps = root_steps()

    def run(number):
        for _ in range(number):
            next(steps, None)

    met, phase1, phase2, phase3 = {}, {}, {}, []
    half_recv, whole_recv = (s1a, s1b), (p1a, p1b)

    def axis(i):
        return (xs[0], xs[2]) if i == 0 else (ys[0], ys[2])

    def spot(i, plane, k):
        return g_own.at[plane, :, (x + k) % NX] if i == 0 else g_own.at[plane, (y + k) % NY]

    for i, j in chunks:
        at = pl.ds(planes(i, j), PC)
        part = grad_part(i, j, c)
        core[i, j].wait_recv()
        g_own[at] = part + core_recv[at]
        low, high = planes(i, j), planes(i, j) + 1
        plus, minus = axis(i)
        met[i, j] = [
            copy(spot(i, low, 2), half_recv[i].at[0, j], plus),
            copy(spot(i, high, 2), half_recv[i].at[1, j], minus),
        ]
        phase1[i, j] = [
            copy(spot(i, high, 1), whole_recv[i].at[0, 2 * j + 1], plus),
            copy(spot(i, low, 3), whole_recv[i].at[1, 2 * j], minus),
        ]
        for item in met[i, j] + phase1[i, j]:
            item.start()
    for i, j in chunks:
        low, high = planes(i, j), planes(i, j) + 1
        plus, minus = axis(i)
        for side, (plane, k, to) in enumerate(((low, 1, plus), (high, 3, minus))):
            met[i, j][side].wait_recv()
            there = spot(i, plane, k)
            there[...] = there[...] + half_recv[i][side, j]
            item = copy(there, whole_recv[i].at[side, 2 * j + side], to)
            item.start()
            phase1[i, j].append(item)

    def second(i, j):
        here = pl.ds(j * PC, PC)
        at = pl.ds(planes(i, j), PC)
        for item in phase1[i, j]:
            item.wait_recv()
        got, total = whole_recv[i], (a1, b1)[i]
        mine = g_own[at, :, x] if i == 0 else g_own[at, y]
        total[here] = mine + got[0, here] + got[1, here]
        group = []
        for k in range(1, 4):
            if i == 0:
                item = copy(total.at[here, (y + k) % NY], p2a.at[k - 1, here], ys[k - 1])
            else:
                item = copy(total.at[here, (x + k) % NX], p2b.at[k - 1, here], xs[k - 1])
            item.start()
            group.append(item)
        phase2[i, j] = group

    z_base = [next(recvs) for _ in range(NZ)][0]

    def third(i, j):
        here = pl.ds(j * PC, PC)
        for item in phase2[i, j]:
            item.wait_recv()
        got, total, at = (p2a, a1, y) if i == 0 else (p2b, b1, x)
        r[pl.ds(planes(i, j), PC)] = total[here, at] + got[0, here] + got[1, here] + got[2, here]
        for q in range(PC):
            p = planes(i, j) + q
            item = copy(r.at[p], p3.at[z], dev(jnp.int32(p), y, x, c), recv_sem.at[z_base + z])
            pl.when(z != p)(item.start)
            phase3.append((z != p, item))

    for n, (i, j) in enumerate(chunks):
        second(i, j)
        if n == 1:
            exchange[1].start()
        if n >= LAG:
            third(*chunks[n - LAG])
    for n in range(len(chunks) - LAG, len(chunks)):
        third(*chunks[n])

    exchange[2].start()
    run(HOOKS[0])
    mine = r[z]
    for k in range(1, NZ):
        source = (z + k) % NZ
        pltpu.make_async_remote_copy(
            src_ref=r.at[z], dst_ref=p3.at[source], send_sem=send_sem.at[0],
            recv_sem=recv_sem.at[z_base + source], device_id=partner, device_id_type=MESH,
        ).wait_recv()
        mine = mine + p3[source]
    fin[...] = mine

    gz_base = [next(recvs) for _ in range(8)][0]
    near = c == keeper
    gz = []
    for k in range(4):
        for t in range(2):
            item = copy(
                fin, tile.at[zl, y, x], gather_to(t, k), recv_sem.at[gz_base + 4 * (zl % 2) + k]
            )
            if k == 0:
                sent = jnp.logical_not(jnp.logical_and(near, 2 * c + t == zl))
                pl.when(sent)(item.start)
                gz.append((sent, item))
            else:
                item.start()
                gz.append((None, item))
    swap = copy(fin, fin_other, partner)
    swap.start()

    def keep():
        tile[zl, y, x] = mine

    pl.when(near)(keep)
    run(HOOKS[1])
    for k in range(4):
        for t in range(2):
            source = 2 * c + t
            from_y = jnp.where(c == 0, (y + 4 - k) % NY, y)
            from_x = jnp.where(c == 0, x, (x + 4 - k) % NX)
            item = pltpu.make_async_remote_copy(
                src_ref=fin, dst_ref=tile.at[source, from_y, from_x], send_sem=send_sem.at[0],
                recv_sem=recv_sem.at[gz_base + 4 * t + k], device_id=partner, device_id_type=MESH,
            )
            if k == 0:
                pl.when(jnp.logical_not(jnp.logical_and(near, source == zl)))(item.wait_recv)
            else:
                item.wait_recv()

    ids = [(next(sends), next(recvs)) for _ in range(7)]
    later, forward = [], []
    for side in range(2):
        two = pl.ds(2 * side, 2)
        slabs = [
            tile.at[two, :, (x + 4 - k) % NX] if side == 0 else tile.at[two, (y + 4 - k) % NY]
            for k in range(4)
        ]

        def make(src, to, n):
            return pltpu.make_async_remote_copy(
                src_ref=src, dst_ref=src, send_sem=send_sem.at[ids[n][0]], recv_sem=recv_sem.at[ids[n][1]],
                device_id=to, device_id_type=MESH,
            )

        later.append([make(slabs[0], (xs, ys)[side][k], k) for k in range(3)])
        forward.append([make(slabs[k], partner, 3 + k) for k in range(4)])

    def both(body):
        pl.when(c == 0)(lambda: body(0))
        pl.when(c == 1)(lambda: body(1))

    def gather_later(side):
        for item in later[side]:
            item.start()
        forward[side][0].start()

    def gather_end(side):
        for k in (1, 3, 2):
            later[side][k - 1].wait_recv()
            forward[side][k].start()

    def gather_take(side):
        for k in (0, 1, 3, 2):
            forward[1 - side][k].wait_recv()

    both(gather_later)
    run(HOOKS[2])
    both(gather_end)
    run(HOOKS[3])

    swap.wait_recv()
    low = jnp.where(c == 0, fin[...], fin_other[...])
    high = jnp.where(c == 0, fin_other[...], fin[...])
    grad_out[:, :BLK] = jnp.where(c == 0, low[:4], low[4:])
    grad_out[:, BLK:] = jnp.where(c == 0, high[:4], high[4:])
    both(gather_take)

    t_value = tile[...].reshape(BLK, BLK)
    t_h, t_l = split(t_value)
    t_high[...] = t_h
    t_low[...] = t_l
    at = (f % 32) * 16

    def left():
        dims = (((1,), (1,)), ((), ()))
        rows = pl.ds(pl.multiple_of(at, 16), 16)
        lead_h, lead_l = t_high[rows, :], t_low[rows, :]
        part = dot(lead_h, t_high[...], dims) + dot(lead_h, t_low[...], dims) + dot(lead_l, t_high[...], dims)
        stats_out[...] = stats_in[...] + part * (1.0 / BLK)

    def right():
        dims = (((0,), (0,)), ((), ()))
        columns = pl.ds(pl.multiple_of(at // 128 * 128, 128), 128)
        lead_h, lead_l = t_high[:, columns], t_low[:, columns]
        wide[...] = dot(lead_h, t_high[...], dims) + dot(lead_h, t_low[...], dims) + dot(lead_l, t_high[...], dims)
        part = wide[pl.ds(pl.multiple_of(at % 128, 16), 16), :]
        stats_out[...] = stats_in[...] + part * (1.0 / BLK)

    pl.when(zl % 2 == 0)(left)
    pl.when(zl % 2 == 1)(right)
    run(20)

    for group in [list(core.values()), exchange, [swap]] + list(met.values()) + list(phase1.values()) + list(phase2.values()):
        for item in group:
            item.wait_send()
    for sent, item in phase3 + gz:
        if sent is None:
            item.wait_send()
        else:
            pl.when(sent)(item.wait_send)

    def sent_all(side):
        for item in later[side] + forward[side]:
            item.wait_send()

    both(sent_all)


def deliver(grad_any, stats_any, root_any, grad_to, stats_to, root_to, sem):
    copies = [
        pltpu.make_async_copy(src, dst, sem.at[i])
        for i, (src, dst) in enumerate(((root_any, root_to), (stats_any, stats_to), (grad_any, grad_to)))
    ]
    for item in copies:
        item.start()
    for item in copies:
        item.wait()


def on_device(hidden_act, out_grad, layer_stats, resident_stats, slot_block, layer_refresh):
    vmem = pl.BlockSpec(memory_space=pltpu.VMEM)
    hbm = pl.BlockSpec(memory_space=pltpu.HBM)
    square = (BLK, BLK)
    piece = (8, BLK)
    scratch = [
        pltpu.VMEM(hidden_act.shape, BF16),
        pltpu.VMEM(out_grad.shape, BF16),
        pltpu.VMEM(layer_stats.shape, F32),
        pltpu.VMEM(resident_stats.shape, F32),
        pltpu.SMEM(slot_block.shape, jnp.int32),
        pltpu.SMEM(layer_refresh.shape, jnp.int32),
        pltpu.VMEM((NZ, NY, NX) + piece, F32),
        pltpu.VMEM((NZ, NY, NX) + piece, F32),
        pltpu.VMEM((NZ, NY, NX) + piece, F32),
        pltpu.VMEM((2, 2, NY) + piece, F32),
        pltpu.VMEM((2, 2, NX) + piece, F32),
        pltpu.VMEM((2, 4, NY) + piece, F32),
        pltpu.VMEM((2, 4, NX) + piece, F32),
        pltpu.VMEM((4, NY) + piece, F32),
        pltpu.VMEM((4, NX) + piece, F32),
        pltpu.VMEM((3, 4) + piece, F32),
        pltpu.VMEM((3, 4) + piece, F32),
        pltpu.VMEM((NZ,) + piece, F32),
        pltpu.VMEM((NZ,) + piece, F32),
        pltpu.VMEM(piece, F32),
        pltpu.VMEM(piece, F32),
        pltpu.VMEM((ZL, NY, NX) + piece, F32),
        pltpu.VMEM(square, BF16),
        pltpu.VMEM(square, BF16),
        pltpu.VMEM((128, BLK), F32),
        pltpu.VMEM((2 * HALF + 8, HALF), F32),
        pltpu.VMEM((2 * HALF + 8, HALF), F32),
        pltpu.VMEM(square, F32),
        pltpu.VMEM(square, BF16),
        pltpu.VMEM(square, BF16),
        pltpu.VMEM(square, BF16),
        pltpu.VMEM(square, BF16),
        pltpu.VMEM(square, BF16),
        pltpu.VMEM(square, BF16),
        pltpu.VMEM(square, BF16),
        pltpu.VMEM(square, BF16),
        pltpu.VMEM(square, F32),
        pltpu.VMEM(square, BF16),
        pltpu.VMEM(square, BF16),
        pltpu.SemaphoreType.DMA((6,)),
        pltpu.SemaphoreType.DMA((SEMS,)),
        pltpu.SemaphoreType.DMA((SEMS,)),
    ]
    shapes = (
        jax.ShapeDtypeStruct((4, 1024), F32),
        jax.ShapeDtypeStruct(layer_stats.shape, F32),
        jax.ShapeDtypeStruct((1, BLK, BLK), F32),
    )
    made = pl.pallas_call(
        kernel,
        out_shape=shapes,
        in_specs=[hbm] * 6,
        out_specs=(vmem, vmem, vmem),
        scratch_shapes=scratch,
        compiler_params=pltpu.CompilerParams(
            collective_id=0, has_side_effects=True, vmem_limit_bytes=48 * 1024 * 1024
        ),
        cost_estimate=pl.CostEstimate(flops=10**10, bytes_accessed=10**7, transcendentals=0),
    )(*[
        pltpu.with_memory_space_constraint(value, pltpu.HBM)
        for value in (hidden_act, out_grad, layer_stats, resident_stats, slot_block, layer_refresh)
    ])
    anywhere = pl.BlockSpec(memory_space=pl.ANY)
    return pl.pallas_call(
        deliver,
        out_shape=shapes,
        in_specs=[vmem] * 3,
        out_specs=(anywhere,) * 3,
        scratch_shapes=[pltpu.SemaphoreType.DMA((3,))],
    )(*[pltpu.with_memory_space_constraint(value, pltpu.VMEM) for value in made])


def solution(mesh):
    in_specs = (
        P(("grp", "fsdp"), None),
        P(("grp", "fsdp"), None),
        P(("grp", "fsdp"), None),
        P(("grp", "fsdp"), None, None),
        P(),
        P(),
    )
    out_specs = (P(("grp", "fsdp"), None), P(("grp", "fsdp"), None), P(("grp", "fsdp"), None, None))
    return jax.shard_map(
        on_device, mesh=mesh, in_specs=in_specs, out_specs=out_specs, check_vma=False
    )
```

```python
import jax
import jax.numpy as jnp
from jax import lax
from jax.experimental import pallas as pl
from jax.experimental.pallas import tpu as pltpu
from jax.sharding import PartitionSpec as P

BPL = 16
EPSILON = 0.0001
MESH = pl.DeviceIdType.MESH
F32 = jnp.float32
BF16 = jnp.bfloat16
ZL, NY, NX, NZ = 4, 4, 4, 8
BLK = 512
HALF = 256
ROWS = 256
NCH = 2
PC = 4 // NCH
LAG = 3
HOOKS = (0, 8, 7, 0)
SEMS = 100
CUTS = (400, 408)


def split(value):
    high = value.astype(BF16)
    return high, (value - high.astype(F32)).astype(BF16)


def dot(a, b, dims=(((1,), (0,)), ((), ()))):
    return lax.dot_general(a, b, dims, preferred_element_type=F32)


def kernel(
    hid_any, og_any, stats_any, res_any, slots_any, refresh_any,
    grad_out, stats_out, root_out,
    hid, og, stats_in, res, slot_block, refresh,
    g_send, g_own, core_recv, s1a, s1b, p1a, p1b, a1, b1, p2a, p2b, r, p3, fin, fin_other,
    tile, t_high, t_low, wide, corner, pack, pack_recv,
    m0, m0_h, m0_l, q_h, q_l, r_h, r_l, w_h, w_l, p_f, p_h, p_l,
    in_sem, send_sem, recv_sem,
):
    grp = lax.axis_index("grp")
    f = lax.axis_index("fsdp")
    zl = f // 32
    y = (f // 8) % NY
    x = (f // 2) % NX
    c = f % 2
    z = grp * ZL + zl

    def dev(z_, y_, x_, c_):
        return (z_ // ZL, (z_ % ZL) * 32 + y_ * 8 + x_ * 2 + c_)

    partner = dev(z, y, x, 1 - c)
    xs = [dev(z, y, (x + k) % NX, c) for k in range(1, NX)]
    ys = [dev(z, (y + k) % NY, x, c) for k in range(1, NY)]
    zs = [dev((z + k) % NZ, y, x, c) for k in range(1, NZ)]

    sends = iter(range(SEMS))
    recvs = iter(range(SEMS))

    def copy(src, dst, to, recv=None):
        return pltpu.make_async_remote_copy(
            src_ref=src, dst_ref=dst, send_sem=send_sem.at[next(sends)],
            recv_sem=recv_sem.at[next(recvs)] if recv is None else recv,
            device_id=to, device_id_type=MESH,
        )

    keeper = zl // 2

    def gather_to(t, k):
        to_y = jnp.where(keeper == 0, (y + k) % NY, y)
        to_x = jnp.where(keeper == 0, x, (x + k) % NX)
        return dev(grp * ZL + 2 * c + t, to_y, to_x, keeper)

    def gather_from(t, k):
        from_y = jnp.where(c == 0, (y + 4 - k) % NY, y)
        from_x = jnp.where(c == 0, x, (x + 4 - k) % NX)
        return dev(grp * ZL + 2 * c + t, from_y, from_x, keeper)

    barrier = pltpu.get_barrier_semaphore()
    peers = [partner] + xs + ys + zs
    cross = [dev(grp * ZL + (zl + k) % ZL, y, x, 1 - c) for k in range(1, ZL)]
    peers = peers + cross
    for t in range(2):
        for k in range(1, 4):
            peers.append(gather_to(t, k))
            peers.append(gather_from(t, k))
    for peer in peers:
        pl.semaphore_signal(barrier, inc=1, device_id=peer, device_id_type=MESH)
    loads = [
        pltpu.make_async_copy(src, dst, in_sem.at[i])
        for i, (src, dst) in enumerate([
            (slots_any, slot_block), (refresh_any, refresh), (og_any, og), (hid_any, hid),
            (res_any, res), (stats_any, stats_in),
        ])
    ]
    for load in loads:
        load.start()

    def planes(i, j):
        return 4 * i + j * PC

    def grad_part(i, j, half):
        rows = pl.ds(planes(i, j) * 128, PC * 128)
        columns = pl.ds(pl.multiple_of(half * BLK, BLK), BLK)
        part = dot(hid[:, rows], og[:, columns], (((0,), (0,)), ((), ())))
        return part.reshape(PC, NY, NX, 8, BLK)

    chunks = [(i, j) for j in range(NCH) for i in range(2)]

    loads[0].wait()
    loads[1].wait()
    own = (grp * 128 + f) * 4
    flags = [refresh[slot_block[own + l] // BPL] for l in range(4)]
    count = flags[0] + flags[1] + flags[2] + flags[3]
    pick0 = jnp.int32(0)
    pick1 = jnp.int32(0)
    before = jnp.int32(0)
    for l in range(4):
        pick0 = pick0 + jnp.where(before == 0, flags[l], 0) * l
        pick1 = pick1 + jnp.where(before == 1, flags[l], 0) * l
        before = before + flags[l]
    send_pick = jnp.where(grp == 0, pick1, pick0)
    own_pick = jnp.where(jnp.logical_and(grp == 1, count == 2), pick1, pick0)
    use_recv = count == 0

    loads[2].wait()
    loads[3].wait()
    core = {}
    for i, j in chunks:
        at = pl.ds(planes(i, j), PC)
        g_send[at] = grad_part(i, j, 1 - c)
        core[i, j] = copy(g_send.at[at], core_recv.at[at], partner)

    row = lax.broadcasted_iota(jnp.int32, (HALF, HALF), 0)
    col = lax.broadcasted_iota(jnp.int32, (HALF, HALF), 1)
    loads[4].wait()
    loads[5].wait()
    lower_block = res[send_pick, HALF:, HALF:]
    pack[0:HALF] = res[send_pick, :HALF, HALF:]
    pack[HALF:2 * HALF] = jnp.where(row <= col, res[send_pick, :HALF, :HALF], lower_block)
    diagonal = jnp.sum(jnp.where(row == col, lower_block, 0.0), axis=0, keepdims=True)
    pack[2 * HALF:2 * HALF + 8] = jnp.broadcast_to(diagonal, (8, HALF))
    exchange = []
    for first, last in zip((0,) + CUTS, CUTS + (2 * HALF + 8,)):
        rows = pl.ds(first, last - first)
        exchange.append(copy(pack.at[rows], pack_recv.at[rows], zs[3]))

    pl.semaphore_wait(barrier, len(peers))
    core[0, 0].start()
    exchange[0].start()
    for item in chunks[1:]:
        core[item].start()

    def root_start():
        for item in exchange:
            item.wait_recv()
        eye = (row == col).astype(F32)
        upper = pack_recv[HALF:2 * HALF]
        flipped = upper.T
        off = pack_recv[0:HALF]
        block_a = jnp.where(row <= col, upper, flipped)
        block_d = jnp.where(row > col, upper, flipped)
        block_d = jnp.where(row == col, jnp.broadcast_to(pack_recv[2 * HALF:2 * HALF + 1], (HALF, HALF)), block_d)
        total = jnp.zeros((1, 1), F32)
        for i, j, got in ((0, 0, block_a), (0, 1, off), (1, 0, off.T), (1, 1, block_d)):
            rows, cols = pl.ds(i * HALF, HALF), pl.ds(j * HALF, HALF)
            value = jnp.where(use_recv, got, res[own_pick, rows, cols])
            if i == j:
                value = value + EPSILON * eye
            m0[rows, cols] = value
            total = total + jnp.sum(value * value, axis=(0, 1), keepdims=True)
        zeta = 2.5 / jnp.sqrt(total + 1e-06)
        scale.append(jnp.sqrt(jnp.sqrt(zeta)))
        value = m0[...] * zeta
        m0[...] = value
        put(m0_h, m0_l, slice(None), value)

    scale = []

    def put(high, low, rows, value):
        value_h, value_l = split(value)
        high[rows, :] = value_h
        low[rows, :] = value_l

    def product(ah, al, bh, bl, i, rows):
        cols = pl.ds(i * ROWS, BLK - i * ROWS)
        lead = ah[rows, :]
        value = dot(lead, bh[:, cols]) + dot(lead, bl[:, cols]) + dot(al[rows, :], bh[:, cols])
        if i == 0:
            corner[...] = value[:, ROWS:]
            return value
        return jnp.concatenate([corner[...].T, value], axis=1)

    def ident(i):
        r_ = lax.broadcasted_iota(jnp.int32, (ROWS, BLK), 0) + i * ROWS
        c_ = lax.broadcasted_iota(jnp.int32, (ROWS, BLK), 1)
        return (r_ == c_).astype(F32)

    def step1(i, rows):
        square = product(m0_h, m0_l, m0_h, m0_l, i, rows)
        m = m0[rows, :]
        put(w_h, w_l, rows, (5.0 * m - square) * 0.25)
        put(q_h, q_l, rows, (25.0 * ident(i) - 10.0 * m + square) * 0.0625)

    def step2(i, rows):
        put(r_h, r_l, rows, product(q_h, q_l, q_h, q_l, i, rows))

    def step3(i, rows):
        fifth = product(r_h, r_l, w_h, w_l, i, rows)
        factor = (5.0 * ident(i) - m0[rows, :]) * 0.25
        value = (5.0 * factor - fifth) * 0.25
        p_f[rows, :] = value
        put(p_h, p_l, rows, value)

    def step4(i, rows):
        put(q_h, q_l, rows, product(p_h, p_l, p_h, p_l, i, rows))

    def step5(i, rows):
        put(w_h, w_l, rows, product(p_h, p_l, m0_h, m0_l, i, rows))

    def step6(i, rows):
        fifth = product(r_h, r_l, w_h, w_l, i, rows)
        root_out[0, rows, :] = (5.0 * p_f[rows, :] - fifth) * (0.25 * scale[0])

    def root_steps():
        yield root_start()
        for body in (step1, step2, step3, step4, step5, step2, step6):
            for i in range(BLK // ROWS):
                yield body(i, pl.ds(i * ROWS, ROWS))

    steps = root_steps()

    def run(number):
        for _ in range(number):
            next(steps, None)

    met, phase1, phase2, phase3 = {}, {}, {}, []
    half_recv, whole_recv = (s1a, s1b), (p1a, p1b)

    def axis(i):
        return (xs[0], xs[2]) if i == 0 else (ys[0], ys[2])

    def spot(i, plane, k):
        return g_own.at[plane, :, (x + k) % NX] if i == 0 else g_own.at[plane, (y + k) % NY]

    for i, j in chunks:
        at = pl.ds(planes(i, j), PC)
        part = grad_part(i, j, c)
        core[i, j].wait_recv()
        g_own[at] = part + core_recv[at]
        low, high = planes(i, j), planes(i, j) + 1
        plus, minus = axis(i)
        met[i, j] = [
            copy(spot(i, low, 2), half_recv[i].at[0, j], plus),
            copy(spot(i, high, 2), half_recv[i].at[1, j], minus),
        ]
        phase1[i, j] = [
            copy(spot(i, high, 1), whole_recv[i].at[0, 2 * j + 1], plus),
            copy(spot(i, low, 3), whole_recv[i].at[1, 2 * j], minus),
        ]
        for item in met[i, j] + phase1[i, j]:
            item.start()
    for i, j in chunks:
        low, high = planes(i, j), planes(i, j) + 1
        plus, minus = axis(i)
        for side, (plane, k, to) in enumerate(((low, 1, plus), (high, 3, minus))):
            met[i, j][side].wait_recv()
            there = spot(i, plane, k)
            there[...] = there[...] + half_recv[i][side, j]
            item = copy(there, whole_recv[i].at[side, 2 * j + side], to)
            item.start()
            phase1[i, j].append(item)

    def second(i, j):
        here = pl.ds(j * PC, PC)
        at = pl.ds(planes(i, j), PC)
        for item in phase1[i, j]:
            item.wait_recv()
        got, total = whole_recv[i], (a1, b1)[i]
        mine = g_own[at, :, x] if i == 0 else g_own[at, y]
        total[here] = mine + got[0, here] + got[1, here]
        group = []
        for k in range(1, 4):
            if i == 0:
                item = copy(total.at[here, (y + k) % NY], p2a.at[k - 1, here], ys[k - 1])
            else:
                item = copy(total.at[here, (x + k) % NX], p2b.at[k - 1, here], xs[k - 1])
            item.start()
            group.append(item)
        phase2[i, j] = group

    z_base = [next(recvs) for _ in range(NZ)][0]

    def third(i, j):
        here = pl.ds(j * PC, PC)
        for item in phase2[i, j]:
            item.wait_recv()
        got, total, at = (p2a, a1, y) if i == 0 else (p2b, b1, x)
        r[pl.ds(planes(i, j), PC)] = total[here, at] + got[0, here] + got[1, here] + got[2, here]
        for q in range(PC):
            p = planes(i, j) + q
            item = copy(r.at[p], p3.at[z], dev(jnp.int32(p), y, x, c), recv_sem.at[z_base + z])
            pl.when(z != p)(item.start)
            phase3.append((z != p, item))

    for n, (i, j) in enumerate(chunks):
        second(i, j)
        if n == 1:
            exchange[1].start()
        if n >= LAG:
            third(*chunks[n - LAG])
    for n in range(len(chunks) - LAG, len(chunks)):
        third(*chunks[n])

    exchange[2].start()
    run(HOOKS[0])
    mine = r[z]
    for k in range(1, NZ):
        source = (z + k) % NZ
        pltpu.make_async_remote_copy(
            src_ref=r.at[z], dst_ref=p3.at[source], send_sem=send_sem.at[0],
            recv_sem=recv_sem.at[z_base + source], device_id=partner, device_id_type=MESH,
        ).wait_recv()
        mine = mine + p3[source]
    fin[...] = mine

    gz_base = [next(recvs) for _ in range(8)][0]
    near = c == keeper
    gz = []
    for k in range(4):
        for t in range(2):
            item = copy(
                fin, tile.at[zl, y, x], gather_to(t, k), recv_sem.at[gz_base + 4 * (zl % 2) + k]
            )
            if k == 0:
                sent = jnp.logical_not(jnp.logical_and(near, 2 * c + t == zl))
                pl.when(sent)(item.start)
                gz.append((sent, item))
            else:
                item.start()
                gz.append((None, item))
    swap = copy(fin, fin_other, partner)
    swap.start()

    def keep():
        tile[zl, y, x] = mine

    pl.when(near)(keep)
    run(HOOKS[1])
    for k in range(4):
        for t in range(2):
            source = 2 * c + t
            from_y = jnp.where(c == 0, (y + 4 - k) % NY, y)
            from_x = jnp.where(c == 0, x, (x + 4 - k) % NX)
            item = pltpu.make_async_remote_copy(
                src_ref=fin, dst_ref=tile.at[source, from_y, from_x], send_sem=send_sem.at[0],
                recv_sem=recv_sem.at[gz_base + 4 * t + k], device_id=partner, device_id_type=MESH,
            )
            if k == 0:
                pl.when(jnp.logical_not(jnp.logical_and(near, source == zl)))(item.wait_recv)
            else:
                item.wait_recv()

    ids = [(next(sends), next(recvs)) for _ in range(7)]
    later, forward = [], []
    for side in range(2):
        two = pl.ds(2 * side, 2)
        slabs = [
            tile.at[two, :, (x + 4 - k) % NX] if side == 0 else tile.at[two, (y + 4 - k) % NY]
            for k in range(4)
        ]

        def make(src, to, n):
            return pltpu.make_async_remote_copy(
                src_ref=src, dst_ref=src, send_sem=send_sem.at[ids[n][0]], recv_sem=recv_sem.at[ids[n][1]],
                device_id=to, device_id_type=MESH,
            )

        later.append([make(slabs[0], (xs, ys)[side][k], k) for k in range(3)])
        forward.append([make(slabs[k], partner, 3 + k) for k in range(4)])

    def both(body):
        pl.when(c == 0)(lambda: body(0))
        pl.when(c == 1)(lambda: body(1))

    def gather_later(side):
        for item in later[side]:
            item.start()
        forward[side][0].start()

    def gather_end(side):
        for k in (1, 3, 2):
            later[side][k - 1].wait_recv()
            forward[side][k].start()

    def gather_take(side):
        for k in (0, 1, 3, 2):
            forward[1 - side][k].wait_recv()

    both(gather_later)
    run(HOOKS[2])
    both(gather_end)
    run(HOOKS[3])

    swap.wait_recv()
    low = jnp.where(c == 0, fin[...], fin_other[...])
    high = jnp.where(c == 0, fin_other[...], fin[...])
    grad_out[:, :BLK] = jnp.where(c == 0, low[:4], low[4:])
    grad_out[:, BLK:] = jnp.where(c == 0, high[:4], high[4:])
    both(gather_take)

    t_value = tile[...].reshape(BLK, BLK)
    t_h, t_l = split(t_value)
    t_high[...] = t_h
    t_low[...] = t_l
    at = (f % 32) * 16

    def left():
        dims = (((1,), (1,)), ((), ()))
        rows = pl.ds(pl.multiple_of(at, 16), 16)
        lead_h, lead_l = t_high[rows, :], t_low[rows, :]
        part = dot(lead_h, t_high[...], dims) + dot(lead_h, t_low[...], dims) + dot(lead_l, t_high[...], dims)
        stats_out[...] = stats_in[...] + part * (1.0 / BLK)

    def right():
        dims = (((0,), (0,)), ((), ()))
        columns = pl.ds(pl.multiple_of(at // 128 * 128, 128), 128)
        lead_h, lead_l = t_high[:, columns], t_low[:, columns]
        wide[...] = dot(lead_h, t_high[...], dims) + dot(lead_h, t_low[...], dims) + dot(lead_l, t_high[...], dims)
        part = wide[pl.ds(pl.multiple_of(at % 128, 16), 16), :]
        stats_out[...] = stats_in[...] + part * (1.0 / BLK)

    pl.when(zl % 2 == 0)(left)
    pl.when(zl % 2 == 1)(right)
    run(20)

    for group in [list(core.values()), exchange, [swap]] + list(met.values()) + list(phase1.values()) + list(phase2.values()):
        for item in group:
            item.wait_send()
    for sent, item in phase3 + gz:
        if sent is None:
            item.wait_send()
        else:
            pl.when(sent)(item.wait_send)

    def sent_all(side):
        for item in later[side] + forward[side]:
            item.wait_send()

    both(sent_all)


def deliver(grad_any, stats_any, root_any, grad_to, stats_to, root_to, sem):
    copies = [
        pltpu.make_async_copy(src, dst, sem.at[i])
        for i, (src, dst) in enumerate(((root_any, root_to), (stats_any, stats_to), (grad_any, grad_to)))
    ]
    for item in copies:
        item.start()
    for item in copies:
        item.wait()


def on_device(hidden_act, out_grad, layer_stats, resident_stats, slot_block, layer_refresh):
    vmem = pl.BlockSpec(memory_space=pltpu.VMEM)
    hbm = pl.BlockSpec(memory_space=pltpu.HBM)
    square = (BLK, BLK)
    piece = (8, BLK)
    scratch = [
        pltpu.VMEM(hidden_act.shape, BF16),
        pltpu.VMEM(out_grad.shape, BF16),
        pltpu.VMEM(layer_stats.shape, F32),
        pltpu.VMEM(resident_stats.shape, F32),
        pltpu.SMEM(slot_block.shape, jnp.int32),
        pltpu.SMEM(layer_refresh.shape, jnp.int32),
        pltpu.VMEM((NZ, NY, NX) + piece, F32),
        pltpu.VMEM((NZ, NY, NX) + piece, F32),
        pltpu.VMEM((NZ, NY, NX) + piece, F32),
        pltpu.VMEM((2, 2, NY) + piece, F32),
        pltpu.VMEM((2, 2, NX) + piece, F32),
        pltpu.VMEM((2, 4, NY) + piece, F32),
        pltpu.VMEM((2, 4, NX) + piece, F32),
        pltpu.VMEM((4, NY) + piece, F32),
        pltpu.VMEM((4, NX) + piece, F32),
        pltpu.VMEM((3, 4) + piece, F32),
        pltpu.VMEM((3, 4) + piece, F32),
        pltpu.VMEM((NZ,) + piece, F32),
        pltpu.VMEM((NZ,) + piece, F32),
        pltpu.VMEM(piece, F32),
        pltpu.VMEM(piece, F32),
        pltpu.VMEM((ZL, NY, NX) + piece, F32),
        pltpu.VMEM(square, BF16),
        pltpu.VMEM(square, BF16),
        pltpu.VMEM((128, BLK), F32),
        pltpu.VMEM((HALF, HALF), F32),
        pltpu.VMEM((2 * HALF + 8, HALF), F32),
        pltpu.VMEM((2 * HALF + 8, HALF), F32),
        pltpu.VMEM(square, F32),
        pltpu.VMEM(square, BF16),
        pltpu.VMEM(square, BF16),
        pltpu.VMEM(square, BF16),
        pltpu.VMEM(square, BF16),
        pltpu.VMEM(square, BF16),
        pltpu.VMEM(square, BF16),
        pltpu.VMEM(square, BF16),
        pltpu.VMEM(square, BF16),
        pltpu.VMEM(square, F32),
        pltpu.VMEM(square, BF16),
        pltpu.VMEM(square, BF16),
        pltpu.SemaphoreType.DMA((6,)),
        pltpu.SemaphoreType.DMA((SEMS,)),
        pltpu.SemaphoreType.DMA((SEMS,)),
    ]
    shapes = (
        jax.ShapeDtypeStruct((4, 1024), F32),
        jax.ShapeDtypeStruct(layer_stats.shape, F32),
        jax.ShapeDtypeStruct((1, BLK, BLK), F32),
    )
    made = pl.pallas_call(
        kernel,
        out_shape=shapes,
        in_specs=[hbm] * 6,
        out_specs=(vmem, vmem, vmem),
        scratch_shapes=scratch,
        compiler_params=pltpu.CompilerParams(
            collective_id=0, has_side_effects=True, vmem_limit_bytes=48 * 1024 * 1024
        ),
        cost_estimate=pl.CostEstimate(flops=10**10, bytes_accessed=10**7, transcendentals=0),
    )(*[
        pltpu.with_memory_space_constraint(value, pltpu.HBM)
        for value in (hidden_act, out_grad, layer_stats, resident_stats, slot_block, layer_refresh)
    ])
    anywhere = pl.BlockSpec(memory_space=pl.ANY)
    return pl.pallas_call(
        deliver,
        out_shape=shapes,
        in_specs=[vmem] * 3,
        out_specs=(anywhere,) * 3,
        scratch_shapes=[pltpu.SemaphoreType.DMA((3,))],
    )(*[pltpu.with_memory_space_constraint(value, pltpu.VMEM) for value in made])


def solution(mesh):
    in_specs = (
        P(("grp", "fsdp"), None),
        P(("grp", "fsdp"), None),
        P(("grp", "fsdp"), None),
        P(("grp", "fsdp"), None, None),
        P(),
        P(),
    )
    out_specs = (P(("grp", "fsdp"), None), P(("grp", "fsdp"), None), P(("grp", "fsdp"), None, None))
    return jax.shard_map(
        on_device, mesh=mesh, in_specs=in_specs, out_specs=out_specs, check_vma=False
    )
```
